128 devices in a mesh: src: 8 (over y, x_lo), rcv: 16 (over z, x_hi, core).
Axes of the slice: x: 4 (x_hi: 2, x_lo: 2; x = x_hi * 2 + x_lo), y: 4, z: 4, core: 2. Of those that a mesh axis runs over, the one named last changes fastest.
Arguments:
- raw: bfloat16 [128, 2048, 512], P(('src', 'rcv')), may hold values from -60 to 60
- quality: int32 [128, 2048], P(('src', 'rcv')), may hold values 0 or 1
- channel_order: int32 [2048], replicated, may hold values from 0 to 2047, each once
- slab_order: int32 [4], replicated, may hold values from 0 to 3, each once
Outputs:
- cross: float32 [2, 64, 2048, 2048], P(None, None, 'src', 'rcv')
The draws below stay inside these ranges and needn't reach their ends.
All inputs are finite; a program needn't handle non-finite values. No bound on the sum of `quality` on one device may be relied on, other than what follows from the above.
Results may differ from the reference program's by a relative error of at most 0.0066.
Values may be sent and summed in bfloat16 or wider, within the bound.
No kernel may reach another device: no remote copies, remote signals or barrier semaphores. Data moves between devices by JAX's collectives and lax.ppermute only.
A program may use at most 128 MiB of HBM per device.

```python
import math
import jax
import jax.numpy as jnp
from jax import lax

C = 2048
WLEN = 512
F = 64
HALF = 12
BAND = 2
SLABS = 4
WIN_SLAB = 32
NW = 128
CB = 16
SB = 256
RB = 128


def draw_raw(key, part):
    k_base = jax.random.fold_in(key, 0)
    k_chan = jax.random.fold_in(key, 1)
    k_win = jax.random.fold_in(key, 2)
    k_level = jax.random.fold_in(key, 4)
    k_sign = jax.random.fold_in(key, 5)
    chan_scale = jnp.exp(jax.random.uniform(k_chan, (1, C, 1), jnp.float32, 0.0, 0.5 * math.log(10.0)))
    win_scale = jnp.exp(jax.random.uniform(k_win, (NW, 1, 1), jnp.float32, 0.0, 0.5 * math.log(10.0)))
    level_size = jax.random.uniform(k_level, (NW, C, 1), jnp.float32, 1.0, 2.5)
    level_sign = jnp.where(jax.random.bernoulli(k_sign, 0.5, (NW, C, 1)), 1.0, -1.0)
    level_shift = level_size * level_sign
    base = jnp.clip(jax.random.normal(k_base, (NW, C, WLEN), jnp.float32), -3.5, 3.5)
    return ((base + level_shift) * chan_scale * win_scale).astype(jnp.bfloat16)


def plant(array, own_key, smallest, high):
    place = [jax.random.randint(jax.random.fold_in(own_key, axis), (), 0, length) for axis, length in enumerate(array.shape)]
    main_axis = array.shape.index(max(array.shape))
    next_to = place[:main_axis] + [(place[main_axis] + 1) % array.shape[main_axis]] + place[main_axis + 1:]
    return array.at[tuple(place)].set(smallest).at[tuple(next_to)].set(high)


def setup_inputs(seed: int = 0) -> dict:
    splits = jax.random.split(jax.random.key(seed), 5)
    return {
        "raw": draw_raw(jax.random.fold_in(splits[4], 71), 0),
        "quality": plant((jax.random.randint(splits[1], (NW, C), 0, 5) < 4).astype(jnp.int32), jax.random.fold_in(splits[1], 1), 0, 1),
        "channel_order": jax.random.permutation(splits[2], C).astype(jnp.int32),
        "slab_order": jax.random.permutation(splits[3], SLABS).astype(jnp.int32),
    }


def band_matrix(length, half_width):
    rows = jnp.arange(length)[:, None]
    cols = jnp.arange(length)[None, :]
    inside = (jnp.abs(rows - cols) <= half_width).astype(jnp.float32)
    return inside / lax.optimization_barrier(jnp.sum(inside, axis=0, keepdims=True))

def fourier_table(samples, bin_count):
    times = jnp.arange(samples, dtype=jnp.int32)[:, None]
    harmonic = jnp.arange(1, bin_count + 1, dtype=jnp.int32)[None, :]
    phase = 2.0 * math.pi / samples * (times * harmonic % samples).astype(jnp.float32)
    return jnp.concatenate([jnp.cos(phase), -jnp.sin(phase)], axis=1).astype(jnp.bfloat16)

def slab_amplitude(slab_order, window_ids):
    count = slab_order.shape[0]
    positions = jnp.arange(count, dtype=jnp.int32)
    slab_ages = lax.optimization_barrier(jnp.sum(jnp.where(slab_order[:, None] == positions[None, :], positions[:, None], 0), axis=0))
    amplitude = 0.5 ** (slab_ages.astype(jnp.float32) / count)
    slab_of = window_ids // WIN_SLAB
    onehot = (slab_of[:, None] == positions[None, :]).astype(jnp.float32)
    return lax.optimization_barrier(jnp.sum(onehot * amplitude[None, :], axis=1))

def whiten_window(window, keep_mask, window_id, slab_order):
    samples = window.shape[1]
    centred = window.astype(jnp.float32)
    centred = centred - lax.optimization_barrier(jnp.mean(centred, axis=1, keepdims=True))
    magnitude = jnp.abs(centred)
    summed = jnp.concatenate([jnp.zeros((magnitude.shape[0], 1), jnp.float32), jnp.cumsum(magnitude, axis=1)], axis=1)
    places = jnp.arange(samples, dtype=jnp.int32)
    upper = jnp.minimum(places + HALF + 1, samples)
    lower = jnp.maximum(places - HALF, 0)
    envelope = (summed[:, upper] - summed[:, lower]) / (upper - lower).astype(jnp.float32)[None, :]
    level = lax.optimization_barrier(jnp.mean(magnitude, axis=1, keepdims=True)) + 1e-06
    normed = (centred / (envelope + 0.25 * level)).astype(jnp.bfloat16)
    spectrum = jnp.dot(normed, fourier_table(samples, F), preferred_element_type=jnp.float32)
    real_part = spectrum[:, :F]
    imag_part = spectrum[:, F:]
    spectral_power = real_part * real_part + imag_part * imag_part
    smooth = jnp.dot(spectral_power, band_matrix(F, BAND), precision=lax.Precision.HIGHEST)
    total = lax.optimization_barrier(jnp.mean(spectral_power, axis=1, keepdims=True)) + 1e-06
    amplitude = slab_amplitude(slab_order, window_id[None])[0]
    weight = keep_mask.astype(jnp.float32)[:, None] * amplitude
    white_scale = weight / jnp.sqrt(smooth + 0.1 * total)
    return (spectrum * jnp.concatenate([white_scale, white_scale], axis=1)).astype(jnp.bfloat16)

def reference(raw, quality, channel_order, slab_order):
    window_total = raw.shape[0]
    keep_all = quality[:, channel_order]
    window_ids = jnp.arange(window_total, dtype=jnp.int32)

    def one_window(items):
        window, keep_mask, window_id = items
        return whiten_window(window[channel_order, :], keep_mask, window_id, slab_order)
    white = lax.map(one_window, (raw, keep_all, window_ids))
    column_ids = jnp.arange(C, dtype=jnp.int32)
    n_src = C // SB
    colpos = column_ids // CB % n_src * SB + column_ids // RB * CB + column_ids % CB
    colpos = colpos.astype(jnp.int32)
    row_side = jnp.transpose(white, (2, 0, 1))
    col_side = jnp.transpose(white[:, colpos, :], (2, 0, 1))
    norm_factor = 1.0 / math.sqrt(window_total)

    def one_bin(items):
        a_real, a_imag, b_real, b_imag = [item.astype(jnp.float32) for item in items]
        hp = lax.Precision.HIGHEST
        real_sum = jnp.dot(a_real.T, b_real, precision=hp) + jnp.dot(a_imag.T, b_imag, precision=hp)
        imag_sum = jnp.dot(a_imag.T, b_real, precision=hp) - jnp.dot(a_real.T, b_imag, precision=hp)
        return (real_sum * norm_factor, imag_sum * norm_factor)
    real_out, imag_out = lax.map(one_bin, (row_side[:F], row_side[F:], col_side[:F], col_side[F:]))
    return jnp.stack([real_out, imag_out])
```

```python
import functools
import math

import jax
import jax.numpy as jnp
import ml_dtypes
import numpy as np
from jax import lax
from jax.experimental import pallas as pl
from jax.experimental.pallas import tpu as pltpu
from jax.sharding import PartitionSpec as P

C, WLEN, F, HALF, BAND, SLABS, WIN_SLAB, NW, CB = 2048, 512, 64, 12, 2, 4, 32, 128, 16
AXES = ("src", "rcv")
GRID = (4, 2, 4, 2, 2)
Y, XL, Z, XH, CORE = range(5)
BF16, F32 = jnp.bfloat16, jnp.float32
ROWS = 256
KC = 8


def tables():
    n = np.arange(WLEN)
    inside = np.abs(n[:, None] - n[None, :]) <= HALF
    harmonic = np.arange(1, F + 1)[None, :]
    phase = 2.0 * math.pi / WLEN * (n[:, None] * harmonic % WLEN)
    dft = np.concatenate([np.cos(phase), -np.sin(phase)], axis=1)
    k = np.arange(F)
    near = np.abs(k[:, None] - k[None, :]) <= BAND
    zero = np.zeros((F, F))
    smooth = np.block([[near, zero], [zero, near]])
    total = np.block([[np.ones((F, F)), zero], [zero, np.ones((F, F))]])
    sums = np.concatenate([smooth, total], axis=1)
    sums = np.concatenate([sums, sums], axis=0)
    bf = ml_dtypes.bfloat16
    return (
        inside.astype(bf),
        (1.0 / inside.sum(0, dtype=np.float64))[None, :].astype(np.float32),
        dft.astype(bf),
        sums.astype(bf),
        (1.0 / np.tile(near.sum(0), 2))[None, :].astype(np.float32),
    )


def whiten_kernel(
    order, slab, wid, raw, quality, inside, inv_count, dft, sums, inv_near, out, white, placed
):
    step = pl.program_id(0)
    x = raw[0].astype(F32)
    centred = x - jnp.sum(x, axis=1, keepdims=True) * (1.0 / WLEN)
    magnitude = jnp.abs(centred)
    level = jnp.sum(magnitude, axis=1, keepdims=True) * (1.0 / WLEN) + 1e-6
    window_sum = jnp.dot(magnitude.astype(BF16), inside[...], preferred_element_type=F32)
    normed = (centred / (window_sum * inv_count[...] + 0.25 * level)).astype(BF16)
    spectrum = jnp.dot(normed, dft[...], preferred_element_type=F32)
    squares = spectrum * spectrum
    power = squares + pltpu.roll(squares, F, 1)
    high = power.astype(BF16)
    low = (power - high.astype(F32)).astype(BF16)
    both = jnp.dot(
        jnp.concatenate([high, low], axis=1), sums[...], preferred_element_type=F32
    )
    total = both[:, 2 * F :] * (1.0 / F) + 1e-6
    amplitude = jnp.float32(0.0)
    for age in range(SLABS):
        amplitude += jnp.where(
            slab[age] == wid[0] // WIN_SLAB, jnp.float32(0.5 ** (age / SLABS)), jnp.float32(0.0)
        )
    eye = (
        lax.broadcasted_iota(jnp.int32, (128, 128), 0)
        == lax.broadcasted_iota(jnp.int32, (128, 128), 1)
    )
    weights = []
    for part in range(ROWS // 128):
        row = quality[pl.ds(step * (ROWS // 128) + part, 1), :].astype(F32)
        weights.append(jnp.sum(jnp.where(eye, row, 0.0), axis=1, keepdims=True))
    weight = jnp.concatenate(weights, axis=0) * amplitude
    scale = weight * lax.rsqrt(both[:, : 2 * F] * inv_near[...] + 0.1 * total)
    white[pl.ds(pl.multiple_of(step * ROWS, ROWS), ROWS), :] = spectrum * scale

    @pl.when(step == pl.num_programs(0) - 1)
    def _():
        def place(group, carry):
            base = pl.multiple_of(group * 16, 16)
            for j in range(16):
                placed[pl.ds(base + j, 1), :] = white[pl.ds(order[base + j], 1), :]
            return carry

        lax.fori_loop(0, C // 16, place, 0)
        out[...] = placed[...].astype(BF16)


def whiten(raw, quality, order, slab, wid):
    inside, inv_count, dft, sums, inv_near = tables()
    whole = lambda a: pl.BlockSpec(a.shape, lambda i, *_: (0, 0))
    consts = [inside, inv_count, dft, sums, inv_near]
    return pl.pallas_call(
        whiten_kernel,
        grid_spec=pltpu.PrefetchScalarGridSpec(
            num_scalar_prefetch=3,
            grid=(C // ROWS,),
            in_specs=[
                pl.BlockSpec((1, ROWS, WLEN), lambda i, *_: (0, i, 0)),
                whole(quality),
                *[whole(a) for a in consts],
            ],
            out_specs=pl.BlockSpec((C, 2 * F), lambda i, *_: (0, 0)),
            scratch_shapes=[pltpu.VMEM((C, 2 * F), F32), pltpu.VMEM((C, 2 * F), F32)],
        ),
        out_shape=jax.ShapeDtypeStruct((C, 2 * F), BF16),
        compiler_params=pltpu.CompilerParams(vmem_limit_bytes=32 << 20),
        name="whiten",
    )(order, slab, wid, raw, quality, *[jnp.asarray(a) for a in consts])


def turn_kernel(received, out, wide, turned):
    wide[...] = received[...].astype(F32)
    for p in range(CB):
        t = wide[pl.ds(p, NW, stride=CB), :].T
        turned[pl.ds(p, F, stride=2 * CB), :] = t[:F]
        turned[pl.ds(CB + p, F, stride=2 * CB), :] = t[F:]
    out[...] = turned[...].astype(BF16)


def turn(received):
    return pl.pallas_call(
        turn_kernel,
        in_specs=[pl.BlockSpec(memory_space=pltpu.VMEM)],
        out_specs=pl.BlockSpec(memory_space=pltpu.VMEM),
        out_shape=jax.ShapeDtypeStruct((F * 2 * CB, NW), BF16),
        scratch_shapes=[pltpu.VMEM((NW * CB, 2 * F), F32), pltpu.VMEM((F * 2 * CB, NW), F32)],
        compiler_params=pltpu.CompilerParams(vmem_limit_bytes=16 << 20),
        name="turn",
    )(received)


def shift(x, axis, amount):
    ids = np.arange(int(np.prod(GRID))).reshape(GRID)
    to = np.roll(ids, -amount, axis=axis)
    return lax.ppermute(x, AXES, [(int(a), int(b)) for a, b in zip(ids.ravel(), to.ravel())])


def gather_ring(x, ring, pair):
    half = x.shape[0] // 2
    other = shift(x, pair, 1)
    found = []
    for flip, block in ((0, x), (1, other)):
        after = shift(block, ring, 1)
        before = shift(block, ring, -1)
        low = shift(after[:half], ring, 1)
        high = shift(before[half:], ring, -1)
        found += [(0, flip, block), (1, flip, after), (3, flip, before), (2, flip, low, high)]
    return found


def product_kernel(meta, *refs, row_parts, col_parts):
    step = pl.program_id(0)
    n_in = sum(row_parts) + sum(col_parts)
    inputs, (out, a, b) = list(refs[:n_in]), refs[n_in:]
    half_steps = pl.num_programs(0) // 2

    def put_row(block, offset):
        a[:, pl.ds(offset, CB), 0:NW] = block[:, 0:CB, :]
        a[:, pl.ds(offset, CB), NW : 2 * NW] = block[:, CB : 2 * CB, :]

    def put_col(block, offset):
        re, im = block[:, 0:CB, :], block[:, CB : 2 * CB, :]
        b[:, pl.ds(offset, CB), 0:NW] = re
        b[:, pl.ds(offset, CB), NW : 2 * NW] = im
        b[:, pl.ds(128 + offset, CB), 0:NW] = -im
        b[:, pl.ds(128 + offset, CB), NW : 2 * NW] = re

    position = 0
    for put, parts in ((put_row, row_parts), (put_col, col_parts)):
        for count in parts:
            offset = pl.multiple_of(meta[position] * CB, CB)
            position += 1
            if count == 1:
                put(inputs.pop(0), offset)
            else:
                low, high = inputs.pop(0), inputs.pop(0)
                pl.when(step < half_steps)(functools.partial(put, low, offset))
                pl.when(step >= half_steps)(functools.partial(put, high, offset))
    factor = 1.0 / math.sqrt(NW)
    for k in range(KC):
        o = lax.dot_general(
            a[k], b[k], (((1,), (1,)), ((), ())), preferred_element_type=F32
        )
        out[0, k] = o[:, :128] * factor
        out[1, k] = o[:, 128:] * factor


def product(meta, rows, cols):
    steps = F // KC
    arrays, specs = [], []
    for group in rows + cols:
        for index, array in enumerate(group):
            array = array.reshape(-1, 2 * CB, NW)
            if len(group) == 1:
                index_map = lambda i, m: (i, 0, 0)
            elif index == 0:
                index_map = lambda i, m: (jnp.minimum(i, steps // 2 - 1), 0, 0)
            else:
                index_map = lambda i, m: (jnp.maximum(i - steps // 2, 0), 0, 0)
            arrays.append(array)
            specs.append(pl.BlockSpec((KC, 2 * CB, NW), index_map))
    return pl.pallas_call(
        functools.partial(
            product_kernel,
            row_parts=[len(g) for g in rows],
            col_parts=[len(g) for g in cols],
        ),
        grid_spec=pltpu.PrefetchScalarGridSpec(
            num_scalar_prefetch=1,
            grid=(steps,),
            in_specs=specs,
            out_specs=pl.BlockSpec((2, KC, 256, 128), lambda i, m: (0, i, 0, 0)),
            scratch_shapes=[pltpu.VMEM((KC, 256, 256), BF16), pltpu.VMEM((KC, 256, 256), BF16)],
        ),
        out_shape=jax.ShapeDtypeStruct((2, F, 256, 128), F32),
        compiler_params=pltpu.CompilerParams(vmem_limit_bytes=40 << 20),
        name="product",
    )(meta, *arrays)


def body(raw, quality, channel_order, slab_order):
    src, rcv = lax.axis_index("src"), lax.axis_index("rcv")
    wid = (src * 16 + rcv).astype(jnp.int32).reshape(1)
    spectra = whiten(raw, quality.reshape(16, 128), channel_order, slab_order, wid)
    received = lax.all_to_all(
        spectra.reshape(NW, CB, 2 * F), AXES, split_axis=0, concat_axis=0, tiled=True
    )
    mine = turn(received.reshape(NW * CB, 2 * F))

    y, xl = src // 2, src % 2
    z, xh, core = rcv // 4, rcv // 2 % 2, rcv % 2
    rows, cols, meta = [], [], []
    for ring, flip, *blocks in gather_ring(mine, Z, XH):
        at = (z - ring) % 4 * 4 + (xh + flip) % 2 * 2
        rows.append(blocks)
        meta.append(at + core)
        rows.append([shift(block, CORE, 1) for block in blocks])
        meta.append(at + 1 - core)
    for ring, flip, *blocks in gather_ring(mine, Y, XL):
        cols.append(blocks)
        meta.append((y - ring) % 4 * 2 + (xl + flip) % 2)
    return product(jnp.stack(meta).astype(jnp.int32), rows, cols)


def solution(mesh):
    in_specs = (P(("src", "rcv"), None, None), P(("src", "rcv"), None), P(), P())
    out_specs = P(None, None, "src", "rcv")
    return jax.shard_map(body, mesh=mesh, in_specs=in_specs, out_specs=out_specs, check_vma=False)
```

```python
import functools
import math

import jax
import jax.numpy as jnp
import ml_dtypes
import numpy as np
from jax import lax
from jax.experimental import pallas as pl
from jax.experimental.pallas import tpu as pltpu
from jax.sharding import PartitionSpec as P

C, WLEN, F, HALF, BAND, SLABS, WIN_SLAB, NW, CB = 2048, 512, 64, 12, 2, 4, 32, 128, 16
AXES = ("src", "rcv")
GRID = (4, 2, 4, 2, 2)
Y, XL, Z, XH, CORE = range(5)
BF16, F32 = jnp.bfloat16, jnp.float32
ROWS = 256
KC = 8


def dft_table():
    n = np.arange(WLEN)[:, None]
    phase = 2.0 * math.pi / WLEN * (n * np.arange(1, F + 1)[None, :] % WLEN)
    table = np.concatenate([np.cos(phase), -np.sin(phase)], axis=1)
    return jnp.asarray(table.astype(ml_dtypes.bfloat16))


def iotas(shape):
    return lax.broadcasted_iota(jnp.int32, shape, 0), lax.broadcasted_iota(jnp.int32, shape, 1)


def make_tables(inside, sums):
    row, col = iotas((WLEN, WLEN))
    inside[...] = jnp.where(jnp.abs(row - col) <= HALF, 1.0, 0.0).astype(BF16)
    row, col = iotas((4 * F, 4 * F))
    same = (row // F) % 2 == (col // F) % 2
    near = (jnp.abs(row % F - col % F) <= BAND) | (col >= 2 * F)
    sums[...] = jnp.where(same & near, 1.0, 0.0).astype(BF16)


def inverse_count(length, half_width, period):
    place = iotas((1, length))[1] % period
    upper = jnp.minimum(place + half_width + 1, period)
    return 1.0 / (upper - jnp.maximum(place - half_width, 0)).astype(F32)


def whiten_kernel(order, slab, wid, raw, quality, dft, out, white, placed, inside, sums):
    step = pl.program_id(0)
    pl.when(step == 0)(functools.partial(make_tables, inside, sums))
    x = raw[0].astype(F32)
    centred = x - jnp.sum(x, axis=1, keepdims=True) * (1.0 / WLEN)
    magnitude = jnp.abs(centred)
    level = jnp.sum(magnitude, axis=1, keepdims=True) * (1.0 / WLEN) + 1e-6
    window_sum = jnp.dot(magnitude.astype(BF16), inside[...], preferred_element_type=F32)
    normed = (centred / (window_sum * inverse_count(WLEN, HALF, WLEN) + 0.25 * level)).astype(BF16)
    spectrum = jnp.dot(normed, dft[...], preferred_element_type=F32)
    squares = spectrum * spectrum
    power = squares + pltpu.roll(squares, F, 1)
    high = power.astype(BF16)
    low = (power - high.astype(F32)).astype(BF16)
    both = jnp.dot(
        jnp.concatenate([high, low], axis=1), sums[...], preferred_element_type=F32
    )
    total = both[:, 2 * F :] * (1.0 / F) + 1e-6
    amplitude = jnp.float32(0.0)
    for age in range(SLABS):
        amplitude += jnp.where(
            slab[age] == wid[0] // WIN_SLAB, jnp.float32(0.5 ** (age / SLABS)), jnp.float32(0.0)
        )
    eye = (
        lax.broadcasted_iota(jnp.int32, (128, 128), 0)
        == lax.broadcasted_iota(jnp.int32, (128, 128), 1)
    )
    weights = []
    for part in range(ROWS // 128):
        row = quality[pl.ds(step * (ROWS // 128) + part, 1), :].astype(F32)
        weights.append(jnp.sum(jnp.where(eye, row, 0.0), axis=1, keepdims=True))
    weight = jnp.concatenate(weights, axis=0) * amplitude
    scale = weight * lax.rsqrt(both[:, : 2 * F] * inverse_count(2 * F, BAND, F) + 0.1 * total)
    white[pl.ds(pl.multiple_of(step * ROWS, ROWS), ROWS), :] = spectrum * scale

    @pl.when(step == pl.num_programs(0) - 1)
    def _():
        def place(group, carry):
            base = pl.multiple_of(group * 16, 16)
            for j in range(16):
                placed[pl.ds(base + j, 1), :] = white[pl.ds(order[base + j], 1), :]
            return carry

        lax.fori_loop(0, C // 16, place, 0)
        out[...] = placed[...].astype(BF16)


def whiten(raw, quality, order, slab, wid):
    whole = lambda shape: pl.BlockSpec(shape, lambda i, *_: (0, 0))
    return pl.pallas_call(
        whiten_kernel,
        grid_spec=pltpu.PrefetchScalarGridSpec(
            num_scalar_prefetch=3,
            grid=(C // ROWS,),
            in_specs=[
                pl.BlockSpec((1, ROWS, WLEN), lambda i, *_: (0, i, 0)),
                whole(quality.shape),
                whole((WLEN, 2 * F)),
            ],
            out_specs=whole((C, 2 * F)),
            scratch_shapes=[
                pltpu.VMEM((C, 2 * F), F32),
                pltpu.VMEM((C, 2 * F), F32),
                pltpu.VMEM((WLEN, WLEN), BF16),
                pltpu.VMEM((4 * F, 4 * F), BF16),
            ],
        ),
        out_shape=jax.ShapeDtypeStruct((C, 2 * F), BF16),
        compiler_params=pltpu.CompilerParams(vmem_limit_bytes=58 << 20),
        name="whiten",
    )(order, slab, wid, raw, quality, dft_table())


def turn_kernel(received, out, wide, turned):
    wide[...] = received[...].astype(F32)
    for p in range(CB):
        t = wide[pl.ds(p, NW, stride=CB), :].T
        turned[pl.ds(p, F, stride=2 * CB), :] = t[:F]
        turned[pl.ds(CB + p, F, stride=2 * CB), :] = t[F:]
    out[...] = turned[...].astype(BF16)


def turn(received):
    return pl.pallas_call(
        turn_kernel,
        in_specs=[pl.BlockSpec(memory_space=pltpu.VMEM)],
        out_specs=pl.BlockSpec(memory_space=pltpu.VMEM),
        out_shape=jax.ShapeDtypeStruct((F * 2 * CB, NW), BF16),
        scratch_shapes=[pltpu.VMEM((NW * CB, 2 * F), F32), pltpu.VMEM((F * 2 * CB, NW), F32)],
        compiler_params=pltpu.CompilerParams(vmem_limit_bytes=16 << 20),
        name="turn",
    )(received)


def shift(x, axis, amount):
    ids = np.arange(int(np.prod(GRID))).reshape(GRID)
    to = np.roll(ids, -amount, axis=axis)
    return lax.ppermute(x, AXES, [(int(a), int(b)) for a, b in zip(ids.ravel(), to.ravel())])


def gather_ring(x, ring, pair):
    half = x.shape[0] // 2
    other = shift(x, pair, 1)
    found = []
    for flip, block in ((0, x), (1, other)):
        after = shift(block, ring, 1)
        before = shift(block, ring, -1)
        low = shift(after[:half], ring, 1)
        high = shift(before[half:], ring, -1)
        found += [(0, flip, block), (1, flip, after), (3, flip, before), (2, flip, low, high)]
    return found


def product_kernel(meta, *refs, row_parts, col_parts):
    step = pl.program_id(0)
    n_in = sum(row_parts) + sum(col_parts)
    inputs, (out, a, b) = list(refs[:n_in]), refs[n_in:]
    half_steps = pl.num_programs(0) // 2

    def put_row(block, offset):
        a[:, pl.ds(offset, CB), 0:NW] = block[:, 0:CB, :]
        a[:, pl.ds(offset, CB), NW : 2 * NW] = block[:, CB : 2 * CB, :]

    def put_col(block, offset):
        re, im = block[:, 0:CB, :], block[:, CB : 2 * CB, :]
        b[:, pl.ds(offset, CB), 0:NW] = re
        b[:, pl.ds(offset, CB), NW : 2 * NW] = im
        b[:, pl.ds(128 + offset, CB), 0:NW] = -im
        b[:, pl.ds(128 + offset, CB), NW : 2 * NW] = re

    position = 0
    for put, parts in ((put_row, row_parts), (put_col, col_parts)):
        for count in parts:
            offset = pl.multiple_of(meta[position] * CB, CB)
            position += 1
            if count == 1:
                put(inputs.pop(0), offset)
            else:
                low, high = inputs.pop(0), inputs.pop(0)
                pl.when(step < half_steps)(functools.partial(put, low, offset))
                pl.when(step >= half_steps)(functools.partial(put, high, offset))
    factor = 1.0 / math.sqrt(NW)
    for k in range(KC):
        o = lax.dot_general(
            a[k], b[k], (((1,), (1,)), ((), ())), preferred_element_type=F32
        )
        out[0, k] = o[:, :128] * factor
        out[1, k] = o[:, 128:] * factor


def product(meta, rows, cols):
    steps = F // KC
    arrays, specs = [], []
    for group in rows + cols:
        for index, array in enumerate(group):
            array = array.reshape(-1, 2 * CB, NW)
            if len(group) == 1:
                index_map = lambda i, m: (i, 0, 0)
            elif index == 0:
                index_map = lambda i, m: (jnp.minimum(i, steps // 2 - 1), 0, 0)
            else:
                index_map = lambda i, m: (jnp.maximum(i - steps // 2, 0), 0, 0)
            arrays.append(array)
            specs.append(pl.BlockSpec((KC, 2 * CB, NW), index_map))
    return pl.pallas_call(
        functools.partial(
            product_kernel,
            row_parts=[len(g) for g in rows],
            col_parts=[len(g) for g in cols],
        ),
        grid_spec=pltpu.PrefetchScalarGridSpec(
            num_scalar_prefetch=1,
            grid=(steps,),
            in_specs=specs,
            out_specs=pl.BlockSpec((2, KC, 256, 128), lambda i, m: (0, i, 0, 0)),
            scratch_shapes=[pltpu.VMEM((KC, 256, 256), BF16), pltpu.VMEM((KC, 256, 256), BF16)],
        ),
        out_shape=jax.ShapeDtypeStruct((2, F, 256, 128), F32),
        compiler_params=pltpu.CompilerParams(vmem_limit_bytes=58 << 20),
        name="product",
    )(meta, *arrays)


def body(raw, quality, channel_order, slab_order):
    src, rcv = lax.axis_index("src"), lax.axis_index("rcv")
    wid = (src * 16 + rcv).astype(jnp.int32).reshape(1)
    spectra = whiten(raw, quality.reshape(16, 128), channel_order, slab_order, wid)
    received = lax.all_to_all(
        spectra.reshape(NW, CB, 2 * F), AXES, split_axis=0, concat_axis=0, tiled=True
    )
    mine = turn(received.reshape(NW * CB, 2 * F))

    y, xl = src // 2, src % 2
    z, xh, core = rcv // 4, rcv // 2 % 2, rcv % 2
    rows, cols, meta = [], [], []
    for ring, flip, *blocks in gather_ring(mine, Z, XH):
        at = (z - ring) % 4 * 4 + (xh + flip) % 2 * 2
        rows.append(blocks)
        meta.append(at + core)
        rows.append([shift(block, CORE, 1) for block in blocks])
        meta.append(at + 1 - core)
    for ring, flip, *blocks in gather_ring(mine, Y, XL):
        cols.append(blocks)
        meta.append((y - ring) % 4 * 2 + (xl + flip) % 2)
    return product(jnp.stack(meta).astype(jnp.int32), rows, cols)


def solution(mesh):
    in_specs = (P(("src", "rcv"), None, None), P(("src", "rcv"), None), P(), P())
    out_specs = P(None, None, "src", "rcv")
    return jax.shard_map(body, mesh=mesh, in_specs=in_specs, out_specs=out_specs, check_vma=False)
```

```python
import functools
import math

import jax
import jax.numpy as jnp
import ml_dtypes
import numpy as np
from jax import lax
from jax.experimental import pallas as pl
from jax.experimental.pallas import tpu as pltpu
from jax.sharding import PartitionSpec as P

C, WLEN, F, HALF, BAND, SLABS, WIN_SLAB, NW, CB = 2048, 512, 64, 12, 2, 4, 32, 128, 16
AXES = ("src", "rcv")
GRID = (4, 2, 4, 2, 2)
Y, XL, Z, XH, CORE = range(5)
BF16, F32 = jnp.bfloat16, jnp.float32
ROWS = 256
KC = 8
XL_BIT, XH_BIT = 16, 2
SENT = 3 * CB
HALF_ROWS = F * 2 * CB


def dft_table():
    n = np.arange(WLEN)[:, None]
    phase = 2.0 * math.pi / WLEN * (n * np.arange(1, F + 1)[None, :] % WLEN)
    table = np.concatenate([np.cos(phase), -np.sin(phase)], axis=1)
    return jnp.asarray(table.astype(ml_dtypes.bfloat16))


def iotas(shape):
    return lax.broadcasted_iota(jnp.int32, shape, 0), lax.broadcasted_iota(jnp.int32, shape, 1)


def make_tables(inside, sums):
    row, col = iotas((WLEN, WLEN))
    inside[...] = jnp.where(jnp.abs(row - col) <= HALF, 1.0, 0.0).astype(BF16)
    row, col = iotas((4 * F, 4 * F))
    same = ((row ^ col) & F) == 0
    near = (jnp.abs((row & (F - 1)) - (col & (F - 1))) <= BAND) | (col >= 2 * F)
    sums[...] = jnp.where(same & near, 1.0, 0.0).astype(BF16)


def inverse_count(length, half_width, period):
    place = iotas((1, length))[1] & (period - 1)
    upper = jnp.minimum(place + half_width + 1, period)
    return 1.0 / (upper - jnp.maximum(place - half_width, 0)).astype(F32)


def whiten_kernel(order, slab, wid, raw, quality, dft, out, white, placed, inside, sums):
    step = pl.program_id(0)
    pl.when(step == 0)(functools.partial(make_tables, inside, sums))
    x = raw[0].astype(F32)
    centred = x - jnp.sum(x, axis=1, keepdims=True) * (1.0 / WLEN)
    magnitude = jnp.abs(centred)
    level = jnp.sum(magnitude, axis=1, keepdims=True) * (1.0 / WLEN) + 1e-6
    window_sum = jnp.dot(magnitude.astype(BF16), inside[...], preferred_element_type=F32)
    normed = (centred / (window_sum * inverse_count(WLEN, HALF, WLEN) + 0.25 * level)).astype(BF16)
    spectrum = jnp.dot(normed, dft[...], preferred_element_type=F32)
    squares = spectrum * spectrum
    power = squares + pltpu.roll(squares, F, 1)
    high = power.astype(BF16)
    low = (power - high.astype(F32)).astype(BF16)
    both = jnp.dot(
        jnp.concatenate([high, low], axis=1), sums[...], preferred_element_type=F32
    )
    total = both[:, 2 * F :] * (1.0 / F) + 1e-6
    amplitude = jnp.float32(0.0)
    for age in range(SLABS):
        amplitude += jnp.where(
            slab[age] == wid[0] // WIN_SLAB, jnp.float32(0.5 ** (age / SLABS)), jnp.float32(0.0)
        )
    eye = (
        lax.broadcasted_iota(jnp.int32, (128, 128), 0)
        == lax.broadcasted_iota(jnp.int32, (128, 128), 1)
    )
    weights = []
    for part in range(ROWS // 128):
        row = quality[pl.ds(step * (ROWS // 128) + part, 1), :].astype(F32)
        weights.append(jnp.sum(jnp.where(eye, row, 0.0), axis=1, keepdims=True))
    weight = jnp.concatenate(weights, axis=0) * amplitude
    scale = weight * lax.rsqrt(both[:, : 2 * F] * inverse_count(2 * F, BAND, F) + 0.1 * total)
    white[pl.ds(pl.multiple_of(step * ROWS, ROWS), ROWS), :] = spectrum * scale

    @pl.when(step == pl.num_programs(0) - 1)
    def _():
        def place(owner, carry):
            base = owner * CB
            for j in range(CB):
                placed[pl.ds(j, 1), :] = white[pl.ds(order[base + j], 1), :]
            block = placed[...].astype(BF16)
            for slot, partner in enumerate((0, XH_BIT, XL_BIT)):
                at = (owner ^ partner) * SENT + slot * CB
                out[pl.ds(pl.multiple_of(at, CB), CB), :] = block
            return carry

        lax.fori_loop(0, C // CB, place, 0)


def whiten(raw, quality, order, slab, wid):
    whole = lambda shape: pl.BlockSpec(shape, lambda i, *_: (0, 0))
    return pl.pallas_call(
        whiten_kernel,
        grid_spec=pltpu.PrefetchScalarGridSpec(
            num_scalar_prefetch=3,
            grid=(C // ROWS,),
            in_specs=[
                pl.BlockSpec((1, ROWS, WLEN), lambda i, *_: (0, i, 0)),
                whole(quality.shape),
                whole((WLEN, 2 * F)),
            ],
            out_specs=whole((NW * SENT, 2 * F)),
            scratch_shapes=[
                pltpu.VMEM((C, 2 * F), F32),
                pltpu.VMEM((CB, 2 * F), F32),
                pltpu.VMEM((WLEN, WLEN), BF16),
                pltpu.VMEM((4 * F, 4 * F), BF16),
            ],
        ),
        out_shape=jax.ShapeDtypeStruct((NW * SENT, 2 * F), BF16),
        compiler_params=pltpu.CompilerParams(vmem_limit_bytes=58 << 20),
        name="whiten",
    )(order, slab, wid, raw, quality, dft_table())


def turn_kernel(received, row_out, col_out, wide, turned):
    wide[...] = received[...].astype(F32)
    for slot in range(3):
        for p in range(CB):
            t = wide[pl.ds(slot * CB + p, NW, stride=SENT), :].T
            turned[pl.ds(p, F, stride=2 * CB), :] = t[:F]
            turned[pl.ds(CB + p, F, stride=2 * CB), :] = t[F:]
        block = turned[...].astype(BF16)
        if slot == 0:
            row_out[0:HALF_ROWS, :] = block
            col_out[0:HALF_ROWS, :] = block
        else:
            (row_out if slot == 1 else col_out)[HALF_ROWS:, :] = block


def turn(received):
    shape = jax.ShapeDtypeStruct((2 * HALF_ROWS, NW), BF16)
    return pl.pallas_call(
        turn_kernel,
        in_specs=[pl.BlockSpec(memory_space=pltpu.VMEM)],
        out_specs=[pl.BlockSpec(memory_space=pltpu.VMEM)] * 2,
        out_shape=[shape, shape],
        scratch_shapes=[pltpu.VMEM((NW * SENT, 2 * F), F32), pltpu.VMEM((HALF_ROWS, NW), F32)],
        compiler_params=pltpu.CompilerParams(vmem_limit_bytes=24 << 20),
        name="turn",
    )(received)


def shift(x, axis, amount):
    ids = np.arange(int(np.prod(GRID))).reshape(GRID)
    to = np.roll(ids, -amount, axis=axis)
    return lax.ppermute(x, AXES, [(int(a), int(b)) for a, b in zip(ids.ravel(), to.ravel())])


def gather_ring(pair, ring):
    after, before = shift(pair, ring, 1), shift(pair, ring, -1)
    low = shift(after[:HALF_ROWS], ring, 1)
    high = shift(before[HALF_ROWS:], ring, -1)
    return [(pair, 0, (0, 1)), (after, 1, (0, 1)), (before, -1, (0, 1)), (low, 2, (0,)), (high, 2, (1,))]


def exchange_cores(rows, cols):
    arrived = lax.optimization_barrier((*rows[1:3], *cols[1:3]))[:2]
    last = lax.optimization_barrier((*rows[3:], *cols[3:]))[:2]
    return [shift(block, CORE, 1) for block in (rows[0], *arrived, *last)]


def product_kernel(meta, *refs):
    rows, cols, (out, a, b) = refs[:16], refs[16:24], refs[24:]

    def put_row(block, offset):
        a[:, pl.ds(offset, CB), 0:NW] = block[:, 0:CB, :]
        a[:, pl.ds(offset, CB), NW : 2 * NW] = block[:, CB : 2 * CB, :]

    def put_col(block, offset):
        re, im = block[:, 0:CB, :], block[:, CB : 2 * CB, :]
        b[:, pl.ds(offset, CB), 0:NW] = re
        b[:, pl.ds(offset, CB), NW : 2 * NW] = im
        b[:, pl.ds(128 + offset, CB), 0:NW] = -im
        b[:, pl.ds(128 + offset, CB), NW : 2 * NW] = re

    for index, block in enumerate(rows + cols):
        put = put_row if index < len(rows) else put_col
        put(block, pl.multiple_of(meta[index] * CB, CB))
    factor = 1.0 / math.sqrt(NW)
    for k in range(KC):
        o = lax.dot_general(
            a[k], b[k], (((1,), (1,)), ((), ())), preferred_element_type=F32
        )
        out[0, k] = o[:, :128] * factor
        out[1, k] = o[:, 128:] * factor


def product(meta, blocks):
    steps = F // KC
    arrays, specs = [], []
    for block in blocks:
        for half in range(block.shape[0] // HALF_ROWS):
            arrays.append(block.reshape(-1, 2 * CB, NW))
            index_map = lambda i, m, half=half: (i + half * steps, 0, 0)
            specs.append(pl.BlockSpec((KC, 2 * CB, NW), index_map))
    return pl.pallas_call(
        product_kernel,
        grid_spec=pltpu.PrefetchScalarGridSpec(
            num_scalar_prefetch=1,
            grid=(steps,),
            in_specs=specs,
            out_specs=pl.BlockSpec((2, KC, 256, 128), lambda i, m: (0, i, 0, 0)),
            scratch_shapes=[pltpu.VMEM((KC, 256, 256), BF16), pltpu.VMEM((KC, 256, 256), BF16)],
        ),
        out_shape=jax.ShapeDtypeStruct((2, F, 256, 128), F32),
        compiler_params=pltpu.CompilerParams(vmem_limit_bytes=58 << 20),
        name="product",
    )(meta, *arrays)


def body(raw, quality, channel_order, slab_order):
    src, rcv = lax.axis_index("src"), lax.axis_index("rcv")
    wid = (src * 16 + rcv).astype(jnp.int32).reshape(1)
    spectra = whiten(raw, quality.reshape(16, 128), channel_order, slab_order, wid)
    received = lax.all_to_all(
        spectra.reshape(NW, SENT, 2 * F), AXES, split_axis=0, concat_axis=0, tiled=True
    )
    row_pair, col_pair = turn(received.reshape(NW * SENT, 2 * F))

    y, xl = src // 2, src % 2
    z, xh, core = rcv // 4, rcv // 2 % 2, rcv % 2
    rows, cols = gather_ring(row_pair, Z), gather_ring(col_pair, Y)
    others = exchange_cores([r[0] for r in rows], [c[0] for c in cols])
    meta = []
    for which in (core, 1 - core):
        for _, ring, flips in rows:
            meta += [(z - ring) % 4 * 4 + (xh + flip) % 2 * 2 + which for flip in flips]
    for _, ring, flips in cols:
        meta += [(y - ring) % 4 * 2 + (xl + flip) % 2 for flip in flips]
    blocks = [block for block, _, _ in rows] + others + [block for block, _, _ in cols]
    return product(jnp.stack(meta).astype(jnp.int32), blocks)


def solution(mesh):
    in_specs = (P(("src", "rcv"), None, None), P(("src", "rcv"), None), P(), P())
    out_specs = P(None, None, "src", "rcv")
    return jax.shard_map(body, mesh=mesh, in_specs=in_specs, out_specs=out_specs, check_vma=False)
```

```python
import functools
import math

import jax
import jax.numpy as jnp
import ml_dtypes
import numpy as np
from jax import lax
from jax.experimental import pallas as pl
from jax.experimental.pallas import tpu as pltpu
from jax.sharding import PartitionSpec as P

C, WLEN, F, HALF, BAND, SLABS, WIN_SLAB, NW, CB = 2048, 512, 64, 12, 2, 4, 32, 128, 16
AXES = ("src", "rcv")
GRID = (4, 2, 4, 2, 2)
Y, XL, Z, XH, CORE = range(5)
BF16, F32 = jnp.bfloat16, jnp.float32
ROWS = 1024
KC = 32
XL_BIT, XH_BIT = 16, 2
SENT = 3 * CB
HALF_ROWS = F * 2 * CB


def dft_table():
    n = np.arange(WLEN)[:, None]
    phase = 2.0 * math.pi / WLEN * (n * np.arange(1, F + 1)[None, :] % WLEN)
    table = np.concatenate([np.cos(phase), -np.sin(phase)], axis=1)
    return jnp.asarray(table.astype(ml_dtypes.bfloat16))


def iotas(shape):
    return lax.broadcasted_iota(jnp.int32, shape, 0), lax.broadcasted_iota(jnp.int32, shape, 1)


def make_tables(inside, sums):
    row, col = iotas((WLEN, WLEN))
    inside[...] = jnp.where(jnp.abs(row - col) <= HALF, 1.0, 0.0).astype(BF16)
    row, col = iotas((4 * F, 4 * F))
    same = ((row ^ col) & F) == 0
    near = (jnp.abs((row & (F - 1)) - (col & (F - 1))) <= BAND) | (col >= 2 * F)
    sums[...] = jnp.where(same & near, 1.0, 0.0).astype(BF16)


def inverse_count(length, half_width, period):
    place = iotas((1, length))[1] & (period - 1)
    upper = jnp.minimum(place + half_width + 1, period)
    return 1.0 / (upper - jnp.maximum(place - half_width, 0)).astype(F32)


def whiten_kernel(order, slab, wid, raw, quality, dft, out, white, placed, inside, sums):
    step = pl.program_id(0)
    pl.when(step == 0)(functools.partial(make_tables, inside, sums))
    x = raw[0].astype(F32)
    centred = x - jnp.sum(x, axis=1, keepdims=True) * (1.0 / WLEN)
    magnitude = jnp.abs(centred)
    level = jnp.sum(magnitude, axis=1, keepdims=True) * (1.0 / WLEN) + 1e-6
    window_sum = jnp.dot(magnitude.astype(BF16), inside[...], preferred_element_type=F32)
    normed = (centred / (window_sum * inverse_count(WLEN, HALF, WLEN) + 0.25 * level)).astype(BF16)
    spectrum = jnp.dot(normed, dft[...], preferred_element_type=F32)
    squares = spectrum * spectrum
    power = squares + pltpu.roll(squares, F, 1)
    high = power.astype(BF16)
    low = (power - high.astype(F32)).astype(BF16)
    both = jnp.dot(
        jnp.concatenate([high, low], axis=1), sums[...], preferred_element_type=F32
    )
    total = both[:, 2 * F :] * (1.0 / F) + 1e-6
    amplitude = jnp.float32(0.0)
    for age in range(SLABS):
        amplitude += jnp.where(
            slab[age] == wid[0] // WIN_SLAB, jnp.float32(0.5 ** (age / SLABS)), jnp.float32(0.0)
        )
    eye = (
        lax.broadcasted_iota(jnp.int32, (128, 128), 0)
        == lax.broadcasted_iota(jnp.int32, (128, 128), 1)
    )
    weights = []
    for part in range(ROWS // 128):
        row = quality[pl.ds(step * (ROWS // 128) + part, 1), :].astype(F32)
        weights.append(jnp.sum(jnp.where(eye, row, 0.0), axis=1, keepdims=True))
    weight = jnp.concatenate(weights, axis=0) * amplitude
    scale = weight * lax.rsqrt(both[:, : 2 * F] * inverse_count(2 * F, BAND, F) + 0.1 * total)
    white[pl.ds(pl.multiple_of(step * ROWS, ROWS), ROWS), :] = spectrum * scale

    @pl.when(step == pl.num_programs(0) - 1)
    def _():
        def place(owner, carry):
            base = owner * CB
            for j in range(CB):
                placed[pl.ds(j, 1), :] = white[pl.ds(order[base + j], 1), :]
            block = placed[...].astype(BF16)
            for slot, partner in enumerate((0, XH_BIT, XL_BIT)):
                at = (owner ^ partner) * SENT + slot * CB
                out[pl.ds(pl.multiple_of(at, CB), CB), :] = block
            return carry

        lax.fori_loop(0, C // CB, place, 0)


def whiten(raw, quality, order, slab, wid):
    whole = lambda shape: pl.BlockSpec(shape, lambda i, *_: (0, 0))
    return pl.pallas_call(
        whiten_kernel,
        grid_spec=pltpu.PrefetchScalarGridSpec(
            num_scalar_prefetch=3,
            grid=(C // ROWS,),
            in_specs=[
                pl.BlockSpec((1, ROWS, WLEN), lambda i, *_: (0, i, 0)),
                whole(quality.shape),
                whole((WLEN, 2 * F)),
            ],
            out_specs=whole((NW * SENT, 2 * F)),
            scratch_shapes=[
                pltpu.VMEM((C, 2 * F), F32),
                pltpu.VMEM((CB, 2 * F), F32),
                pltpu.VMEM((WLEN, WLEN), BF16),
                pltpu.VMEM((4 * F, 4 * F), BF16),
            ],
        ),
        out_shape=jax.ShapeDtypeStruct((NW * SENT, 2 * F), BF16),
        compiler_params=pltpu.CompilerParams(vmem_limit_bytes=58 << 20),
        name="whiten",
    )(order, slab, wid, raw, quality, dft_table())


def turn_block(wide, first, step, turned):
    for p in range(CB):
        t = wide[pl.ds(first + p, NW, stride=step), :].T
        turned[pl.ds(p, F, stride=2 * CB), :] = t[:F]
        turned[pl.ds(CB + p, F, stride=2 * CB), :] = t[F:]
    return turned[...].astype(BF16)


def turn_two_kernel(received, out, wide, turned):
    wide[...] = received[...].astype(F32).reshape(wide.shape)
    for slot in range(2):
        block = turn_block(wide, slot * CB, 2 * CB, turned)
        out[pl.ds(slot * HALF_ROWS, HALF_ROWS), :] = block


def turn_one_kernel(received, own, out, wide, turned):
    wide[...] = received[...].astype(F32).reshape(wide.shape)
    out[0:HALF_ROWS, :] = own[...]
    out[HALF_ROWS:, :] = turn_block(wide, 0, CB, turned)


def turn_call(kernel, received, slots, first, *own):
    return pl.pallas_call(
        kernel,
        grid=(1,),
        in_specs=[
            pl.BlockSpec((NW, slots * CB, 2 * F), lambda i: (0, first, 0)),
            *[pl.BlockSpec((HALF_ROWS, NW), lambda i: (0, 0)) for _ in own],
        ],
        out_specs=pl.BlockSpec((2 * HALF_ROWS, NW), lambda i: (0, 0)),
        out_shape=jax.ShapeDtypeStruct((2 * HALF_ROWS, NW), BF16),
        scratch_shapes=[
            pltpu.VMEM((NW * slots * CB, 2 * F), F32),
            pltpu.VMEM((HALF_ROWS, NW), F32),
        ],
        compiler_params=pltpu.CompilerParams(vmem_limit_bytes=24 << 20),
        name="turn",
    )(received, *own)


def shift(x, axis, amount):
    ids = np.arange(int(np.prod(GRID))).reshape(GRID)
    to = np.roll(ids, -amount, axis=axis)
    return lax.ppermute(x, AXES, [(int(a), int(b)) for a, b in zip(ids.ravel(), to.ravel())])


def gather_rings(row_pair, col_pair):
    rows = [row_pair, shift(row_pair, Z, 1), shift(row_pair, Z, -1)]
    cols = [col_pair, shift(col_pair, Y, 1), shift(col_pair, Y, -1)]
    others = [shift(row_pair, CORE, 1)]
    halves = (rows[1][:HALF_ROWS], rows[2][HALF_ROWS:])
    halves = lax.optimization_barrier((*halves, *others))[:2]
    for ring, halves in ((Z, halves), (Y, (cols[1][:HALF_ROWS], cols[2][HALF_ROWS:]))):
        far = [shift(half, ring, way) for half, way in zip(halves, (1, -1))]
        (rows if ring == Z else cols).extend(far)
    after = lax.optimization_barrier((*rows[1:3], *cols[1:3]))[0]
    others.append(shift(after, CORE, 1))
    before, _ = lax.optimization_barrier((rows[2], others[1]))
    others.append(shift(before, CORE, 1))
    far = lax.optimization_barrier((*rows[3:], *cols[3:]))[:2]
    others += [shift(block, CORE, 1) for block in far]
    return rows, others, cols


def block_offsets(wid):
    bits = lambda low, size: (wid >> low) & (size - 1)
    y, xl, z, xh, core = bits(5, 4), bits(4, 2), bits(2, 4), bits(1, 2), bits(0, 2)
    held = [(0, 0), (0, 1), (1, 0), (1, 1), (3, 0), (3, 1), (2, 0), (2, 1)]
    rows = [((z - ring) & 3) * 4 + (xh ^ flip) * 2 for ring, flip in held]
    cols = [((y - ring) & 3) * 2 + (xl ^ flip) for ring, flip in held]
    return [at * CB for at in [r + core for r in rows] + [r + 1 - core for r in rows] + cols]


def product_kernel(wid, *refs):
    rows, cols, (out, b) = refs[:16], refs[16:24], refs[24:]
    offsets = [pl.multiple_of(at, CB) for at in block_offsets(wid[0])]
    for block, offset in zip(cols, offsets[16:]):
        re, im = block[:, 0:CB, :], block[:, CB : 2 * CB, :]
        b[:, pl.ds(offset, CB), 0:NW] = re
        b[:, pl.ds(offset, CB), NW : 2 * NW] = im
        b[:, pl.ds(128 + offset, CB), 0:NW] = -im
        b[:, pl.ds(128 + offset, CB), NW : 2 * NW] = re
    factor = 1.0 / math.sqrt(NW)
    for k in range(KC):
        halves = [
            jnp.concatenate([row[k, 0:CB, :], row[k, CB : 2 * CB, :]], axis=1) for row in rows
        ]
        o = lax.dot_general(
            jnp.concatenate(halves, axis=0),
            b[k],
            (((1,), (1,)), ((), ())),
            preferred_element_type=F32,
        )
        o = o * factor
        for index, offset in enumerate(offsets[:16]):
            part = o[index * CB : (index + 1) * CB]
            out[0, k, pl.ds(offset, CB), :] = part[:, :128]
            out[1, k, pl.ds(offset, CB), :] = part[:, 128:]


def product(wid, blocks):
    steps = F // KC
    arrays, specs = [], []
    for block in blocks:
        for half in range(block.shape[0] // HALF_ROWS):
            arrays.append(block.reshape(-1, 2 * CB, NW))
            index_map = lambda i, m, half=half: (i + half * steps, 0, 0)
            specs.append(pl.BlockSpec((KC, 2 * CB, NW), index_map))
    return pl.pallas_call(
        product_kernel,
        grid_spec=pltpu.PrefetchScalarGridSpec(
            num_scalar_prefetch=1,
            grid=(steps,),
            in_specs=specs,
            out_specs=pl.BlockSpec((2, KC, 256, 128), lambda i, m: (0, i, 0, 0)),
            scratch_shapes=[pltpu.VMEM((KC, 256, 256), BF16)],
        ),
        out_shape=jax.ShapeDtypeStruct((2, F, 256, 128), F32),
        compiler_params=pltpu.CompilerParams(vmem_limit_bytes=58 << 20),
        name="product",
    )(wid, *arrays)


def body(raw, quality, channel_order, slab_order):
    src, rcv = lax.axis_index("src"), lax.axis_index("rcv")
    wid = (src * 16 + rcv).astype(jnp.int32).reshape(1)
    spectra = whiten(raw, quality.reshape(16, 128), channel_order, slab_order, wid)
    received = lax.all_to_all(
        spectra.reshape(NW, SENT, 2 * F), AXES, split_axis=0, concat_axis=0, tiled=True
    )
    row_pair = turn_call(turn_two_kernel, received, 2, 0)
    col_pair = turn_call(turn_one_kernel, received, 1, 2, row_pair)
    rows, others, cols = gather_rings(row_pair, col_pair)
    return product(wid, rows + others + cols)


def solution(mesh):
    in_specs = (P(("src", "rcv"), None, None), P(("src", "rcv"), None), P(), P())
    out_specs = P(None, None, "src", "rcv")
    return jax.shard_map(body, mesh=mesh, in_specs=in_specs, out_specs=out_specs, check_vma=False)
```

```python
import functools
import math

import jax
import jax.numpy as jnp
import ml_dtypes
import numpy as np
from jax import lax
from jax.experimental import pallas as pl
from jax.experimental.pallas import tpu as pltpu
from jax.sharding import PartitionSpec as P

C, WLEN, F, HALF, BAND, SLABS, WIN_SLAB, NW, CB = 2048, 512, 64, 12, 2, 4, 32, 128, 16
AXES = ("src", "rcv")
GRID = (4, 2, 4, 2, 2)
Y, XL, Z, XH, CORE = range(5)
BF16, F32 = jnp.bfloat16, jnp.float32
ROWS = 1024
GROUP = 8
KC = 32
XH_BIT = 2
SENT = 2 * CB
HALF_ROWS = F * 2 * CB


def dft_table():
    n = np.arange(WLEN)[:, None]
    phase = 2.0 * math.pi / WLEN * (n * np.arange(1, F + 1)[None, :] % WLEN)
    table = np.concatenate([np.cos(phase), -np.sin(phase)], axis=1)
    return jnp.asarray(table.astype(ml_dtypes.bfloat16))


def iotas(shape):
    return lax.broadcasted_iota(jnp.int32, shape, 0), lax.broadcasted_iota(jnp.int32, shape, 1)


def make_tables(inside, sums):
    row, col = iotas((WLEN, WLEN))
    inside[...] = jnp.where(jnp.abs(row - col) <= HALF, 1.0, 0.0).astype(BF16)
    row, col = iotas((4 * F, 4 * F))
    same = ((row ^ col) & F) == 0
    near = (jnp.abs((row & (F - 1)) - (col & (F - 1))) <= BAND) | (col >= 2 * F)
    sums[...] = jnp.where(same & near, 1.0, 0.0).astype(BF16)


def inverse_count(length, half_width, period):
    place = iotas((1, length))[1] & (period - 1)
    upper = jnp.minimum(place + half_width + 1, period)
    return 1.0 / (upper - jnp.maximum(place - half_width, 0)).astype(F32)


def whiten_kernel(order, slab, wid, raw, quality, dft, out, white, placed, inside, sums):
    step = pl.program_id(0)
    pl.when(step == 0)(functools.partial(make_tables, inside, sums))
    x = raw[0].astype(F32)
    centred = x - jnp.sum(x, axis=1, keepdims=True) * (1.0 / WLEN)
    magnitude = jnp.abs(centred)
    level = jnp.sum(magnitude, axis=1, keepdims=True) * (1.0 / WLEN) + 1e-6
    window_sum = jnp.dot(magnitude.astype(BF16), inside[...], preferred_element_type=F32)
    normed = (centred / (window_sum * inverse_count(WLEN, HALF, WLEN) + 0.25 * level)).astype(BF16)
    spectrum = jnp.dot(normed, dft[...], preferred_element_type=F32)
    squares = spectrum * spectrum
    power = squares + pltpu.roll(squares, F, 1)
    high = power.astype(BF16)
    low = (power - high.astype(F32)).astype(BF16)
    both = jnp.dot(
        jnp.concatenate([high, low], axis=1), sums[...], preferred_element_type=F32
    )
    total = both[:, 2 * F :] * (1.0 / F) + 1e-6
    amplitude = jnp.float32(0.0)
    for age in range(SLABS):
        amplitude += jnp.where(
            slab[age] == wid[0] // WIN_SLAB, jnp.float32(0.5 ** (age / SLABS)), jnp.float32(0.0)
        )
    eye = (
        lax.broadcasted_iota(jnp.int32, (128, 128), 0)
        == lax.broadcasted_iota(jnp.int32, (128, 128), 1)
    )
    weights = []
    for part in range(ROWS // 128):
        row = quality[pl.ds(step * (ROWS // 128) + part, 1), :].astype(F32)
        weights.append(jnp.sum(jnp.where(eye, row, 0.0), axis=1, keepdims=True))
    weight = jnp.concatenate(weights, axis=0) * amplitude
    scale = weight * lax.rsqrt(both[:, : 2 * F] * inverse_count(2 * F, BAND, F) + 0.1 * total)
    white[pl.ds(pl.multiple_of(step * ROWS, ROWS), ROWS), :] = spectrum * scale

    @pl.when(step == pl.num_programs(0) - 1)
    def _():
        def place(group, carry):
            for u in range(GROUP):
                base = (group * GROUP + u) * CB
                for j in range(CB):
                    placed[pl.ds(u * CB + j, 1), :] = white[pl.ds(order[base + j], 1), :]
            for u in range(GROUP):
                owner = group * GROUP + u
                block = placed[pl.ds(u * CB, CB), :].astype(BF16)
                for slot, partner in enumerate((0, XH_BIT)):
                    at = (owner ^ partner) * SENT + slot * CB
                    out[pl.ds(pl.multiple_of(at, CB), CB), :] = block
            return carry

        lax.fori_loop(0, C // CB // GROUP, place, 0)


def whiten(raw, quality, order, slab, wid):
    whole = lambda shape: pl.BlockSpec(shape, lambda i, *_: (0, 0))
    return pl.pallas_call(
        whiten_kernel,
        grid_spec=pltpu.PrefetchScalarGridSpec(
            num_scalar_prefetch=3,
            grid=(C // ROWS,),
            in_specs=[
                pl.BlockSpec((1, ROWS, WLEN), lambda i, *_: (0, i, 0)),
                whole(quality.shape),
                whole((WLEN, 2 * F)),
            ],
            out_specs=whole((NW * SENT, 2 * F)),
            scratch_shapes=[
                pltpu.VMEM((C, 2 * F), F32),
                pltpu.VMEM((GROUP * CB, 2 * F), F32),
                pltpu.VMEM((WLEN, WLEN), BF16),
                pltpu.VMEM((4 * F, 4 * F), BF16),
            ],
        ),
        out_shape=jax.ShapeDtypeStruct((NW * SENT, 2 * F), BF16),
        compiler_params=pltpu.CompilerParams(vmem_limit_bytes=58 << 20),
        name="whiten",
    )(order, slab, wid, raw, quality, dft_table())


def turn_block(wide, first, step, turned):
    for p in range(CB):
        t = wide[pl.ds(first + p, NW, stride=step), :].T
        turned[pl.ds(p, F, stride=2 * CB), :] = t[:F]
        turned[pl.ds(CB + p, F, stride=2 * CB), :] = t[F:]
    return turned[...].astype(BF16)


def turn_kernel(received, pair, own, wide, turned):
    wide[...] = received[...].astype(F32)
    for slot in range(2):
        block = turn_block(wide, slot * CB, SENT, turned)
        pair[pl.ds(slot * HALF_ROWS, HALF_ROWS), :] = block
        if slot == 0:
            own[...] = block


def turn(received):
    return pl.pallas_call(
        turn_kernel,
        in_specs=[pl.BlockSpec(memory_space=pltpu.VMEM)],
        out_specs=[pl.BlockSpec(memory_space=pltpu.VMEM)] * 2,
        out_shape=[
            jax.ShapeDtypeStruct((2 * HALF_ROWS, NW), BF16),
            jax.ShapeDtypeStruct((HALF_ROWS, NW), BF16),
        ],
        scratch_shapes=[pltpu.VMEM((NW * SENT, 2 * F), F32), pltpu.VMEM((HALF_ROWS, NW), F32)],
        compiler_params=pltpu.CompilerParams(vmem_limit_bytes=24 << 20),
        name="turn",
    )(received)


def shift(x, axis, amount):
    ids = np.arange(int(np.prod(GRID))).reshape(GRID)
    to = np.roll(ids, -amount, axis=axis)
    return lax.ppermute(x, AXES, [(int(a), int(b)) for a, b in zip(ids.ravel(), to.ravel())])


def gather_rings(pair, own):
    rows = [pair, shift(pair, Z, 1), shift(pair, Z, -1)]
    partner = shift(own, XL, 1)
    cols = []
    for block, far in ((own, 1), (partner, -1)):
        near = {way: shift(block, Y, way) for way in (1, -1)}
        cols += [block, near[1], near[-1], shift(near[far], Y, far)]
    rows.append(shift(rows[1][:HALF_ROWS], Z, 1))
    rows.append(shift(rows[2][HALF_ROWS:], Z, -1))
    others = [shift(pair, CORE, 1)]
    near = lax.optimization_barrier((*rows[1:3], *cols[1:3], *cols[5:7]))[:2]
    others += [shift(block, CORE, 1) for block in near]
    far = lax.optimization_barrier((*rows[3:], cols[3], cols[7]))[:2]
    others += [shift(block, CORE, 1) for block in far]
    return rows, others, cols


def block_offsets(wid):
    bits = lambda low, size: (wid >> low) & (size - 1)
    y, xl, z, xh, core = bits(5, 4), bits(4, 2), bits(2, 4), bits(1, 2), bits(0, 2)
    held = [(0, 0), (0, 1), (1, 0), (1, 1), (3, 0), (3, 1), (2, 0), (2, 1)]
    rows = [((z - ring) & 3) * 4 + (xh ^ flip) * 2 for ring, flip in held]
    cols = [((y - ring) & 3) * 2 + (xl ^ flip) for flip in (0, 1) for ring in (0, 1, 3, 2)]
    return [at * CB for at in [r + core for r in rows] + [r + 1 - core for r in rows] + cols]


def product_kernel(wid, *refs):
    rows, cols, (out, b) = refs[:16], refs[16:24], refs[24:]
    offsets = [pl.multiple_of(at, CB) for at in block_offsets(wid[0])]
    for block, offset in zip(cols, offsets[16:]):
        re, im = block[:, 0:CB, :], block[:, CB : 2 * CB, :]
        b[:, pl.ds(offset, CB), 0:NW] = re
        b[:, pl.ds(offset, CB), NW : 2 * NW] = im
        b[:, pl.ds(128 + offset, CB), 0:NW] = -im
        b[:, pl.ds(128 + offset, CB), NW : 2 * NW] = re
    factor = 1.0 / math.sqrt(NW)
    for k in range(KC):
        halves = [
            jnp.concatenate([row[k, 0:CB, :], row[k, CB : 2 * CB, :]], axis=1) for row in rows
        ]
        o = lax.dot_general(
            jnp.concatenate(halves, axis=0),
            b[k],
            (((1,), (1,)), ((), ())),
            preferred_element_type=F32,
        )
        o = o * factor
        for index, offset in enumerate(offsets[:16]):
            part = o[index * CB : (index + 1) * CB]
            out[0, k, pl.ds(offset, CB), :] = part[:, :128]
            out[1, k, pl.ds(offset, CB), :] = part[:, 128:]


def product(wid, blocks):
    steps = F // KC
    arrays, specs = [], []
    for block in blocks:
        for half in range(block.shape[0] // HALF_ROWS):
            arrays.append(block.reshape(-1, 2 * CB, NW))
            index_map = lambda i, m, half=half: (i + half * steps, 0, 0)
            specs.append(pl.BlockSpec((KC, 2 * CB, NW), index_map))
    return pl.pallas_call(
        product_kernel,
        grid_spec=pltpu.PrefetchScalarGridSpec(
            num_scalar_prefetch=1,
            grid=(steps,),
            in_specs=specs,
            out_specs=pl.BlockSpec((2, KC, 256, 128), lambda i, m: (0, i, 0, 0)),
            scratch_shapes=[pltpu.VMEM((KC, 256, 256), BF16)],
        ),
        out_shape=jax.ShapeDtypeStruct((2, F, 256, 128), F32),
        compiler_params=pltpu.CompilerParams(vmem_limit_bytes=58 << 20),
        name="product",
    )(wid, *arrays)


def body(raw, quality, channel_order, slab_order):
    src, rcv = lax.axis_index("src"), lax.axis_index("rcv")
    wid = (src * 16 + rcv).astype(jnp.int32).reshape(1)
    spectra = whiten(raw, quality.reshape(16, 128), channel_order, slab_order, wid)
    received = lax.all_to_all(
        spectra.reshape(NW, SENT, 2 * F), AXES, split_axis=0, concat_axis=0, tiled=True
    )
    pair, own = turn(received.reshape(NW * SENT, 2 * F))
    rows, others, cols = gather_rings(pair, own)
    return product(wid, rows + others + cols)


def solution(mesh):
    in_specs = (P(("src", "rcv"), None, None), P(("src", "rcv"), None), P(), P())
    out_specs = P(None, None, "src", "rcv")
    return jax.shard_map(body, mesh=mesh, in_specs=in_specs, out_specs=out_specs, check_vma=False)
```

```python
import functools
import math

import jax
import jax.numpy as jnp
import ml_dtypes
import numpy as np
from jax import lax
from jax.experimental import pallas as pl
from jax.experimental.pallas import tpu as pltpu
from jax.sharding import PartitionSpec as P

C, WLEN, F, HALF, BAND, SLABS, WIN_SLAB, NW, CB = 2048, 512, 64, 12, 2, 4, 32, 128, 16
AXES = ("src", "rcv")
GRID = (4, 2, 4, 2, 2)
Y, XL, Z, XH, CORE = range(5)
BF16, F32 = jnp.bfloat16, jnp.float32
ROWS = 1024
GROUP = 8
KC = 32
OUT_BINS = 8
XH_BIT = 2
SENT = 2 * CB
HALF_ROWS = F * 2 * CB


def dft_table():
    n = np.arange(WLEN)[:, None]
    phase = 2.0 * math.pi / WLEN * (n * np.arange(1, F + 1)[None, :] % WLEN)
    table = np.concatenate([np.cos(phase), -np.sin(phase)], axis=1)
    return jnp.asarray(table.astype(ml_dtypes.bfloat16))


def iotas(shape):
    return lax.broadcasted_iota(jnp.int32, shape, 0), lax.broadcasted_iota(jnp.int32, shape, 1)


def make_tables(inside, sums):
    row, col = iotas((WLEN, WLEN))
    inside[...] = jnp.where(jnp.abs(row - col) <= HALF, 1.0, 0.0).astype(BF16)
    row, col = iotas((4 * F, 4 * F))
    same = ((row ^ col) & F) == 0
    near = (jnp.abs((row & (F - 1)) - (col & (F - 1))) <= BAND) | (col >= 2 * F)
    sums[...] = jnp.where(same & near, 1.0, 0.0).astype(BF16)


def inverse_count(length, half_width, period):
    place = iotas((1, length))[1] & (period - 1)
    upper = jnp.minimum(place + half_width + 1, period)
    return 1.0 / (upper - jnp.maximum(place - half_width, 0)).astype(F32)


def whiten_kernel(order, slab, wid, raw, quality, dft, out, white, placed, inside, sums):
    step = pl.program_id(0)
    pl.when(step == 0)(functools.partial(make_tables, inside, sums))
    x = raw[0].astype(F32)
    centred = x - jnp.sum(x, axis=1, keepdims=True) * (1.0 / WLEN)
    magnitude = jnp.abs(centred)
    level = jnp.sum(magnitude, axis=1, keepdims=True) * (1.0 / WLEN) + 1e-6
    window_sum = jnp.dot(magnitude.astype(BF16), inside[...], preferred_element_type=F32)
    normed = (centred / (window_sum * inverse_count(WLEN, HALF, WLEN) + 0.25 * level)).astype(BF16)
    spectrum = jnp.dot(normed, dft[...], preferred_element_type=F32)
    squares = spectrum * spectrum
    power = squares + pltpu.roll(squares, F, 1)
    high = power.astype(BF16)
    low = (power - high.astype(F32)).astype(BF16)
    both = jnp.dot(
        jnp.concatenate([high, low], axis=1), sums[...], preferred_element_type=F32
    )
    total = both[:, 2 * F :] * (1.0 / F) + 1e-6
    amplitude = jnp.float32(0.0)
    for age in range(SLABS):
        amplitude += jnp.where(
            slab[age] == wid[0] // WIN_SLAB, jnp.float32(0.5 ** (age / SLABS)), jnp.float32(0.0)
        )
    eye = (
        lax.broadcasted_iota(jnp.int32, (128, 128), 0)
        == lax.broadcasted_iota(jnp.int32, (128, 128), 1)
    )
    weights = []
    for part in range(ROWS // 128):
        row = quality[pl.ds(step * (ROWS // 128) + part, 1), :].astype(F32)
        weights.append(jnp.sum(jnp.where(eye, row, 0.0), axis=1, keepdims=True))
    weight = jnp.concatenate(weights, axis=0) * amplitude
    scale = weight * lax.rsqrt(both[:, : 2 * F] * inverse_count(2 * F, BAND, F) + 0.1 * total)
    white[pl.ds(pl.multiple_of(step * ROWS, ROWS), ROWS), :] = spectrum * scale

    @pl.when(step == pl.num_programs(0) - 1)
    def _():
        def place(group, carry):
            for u in range(GROUP):
                base = (group * GROUP + u) * CB
                for j in range(CB):
                    placed[pl.ds(u * CB + j, 1), :] = white[pl.ds(order[base + j], 1), :]
            for u in range(GROUP):
                owner = group * GROUP + u
                block = placed[pl.ds(u * CB, CB), :].astype(BF16)
                for slot, partner in enumerate((0, XH_BIT)):
                    at = (owner ^ partner) * SENT + slot * CB
                    out[pl.ds(pl.multiple_of(at, CB), CB), :] = block
            return carry

        lax.fori_loop(0, C // CB // GROUP, place, 0)


def whiten(raw, quality, order, slab, wid):
    whole = lambda shape: pl.BlockSpec(shape, lambda i, *_: (0, 0))
    return pl.pallas_call(
        whiten_kernel,
        grid_spec=pltpu.PrefetchScalarGridSpec(
            num_scalar_prefetch=3,
            grid=(C // ROWS,),
            in_specs=[
                pl.BlockSpec((1, ROWS, WLEN), lambda i, *_: (0, i, 0)),
                whole(quality.shape),
                whole((WLEN, 2 * F)),
            ],
            out_specs=whole((NW * SENT, 2 * F)),
            scratch_shapes=[
                pltpu.VMEM((C, 2 * F), F32),
                pltpu.VMEM((GROUP * CB, 2 * F), F32),
                pltpu.VMEM((WLEN, WLEN), BF16),
                pltpu.VMEM((4 * F, 4 * F), BF16),
            ],
        ),
        out_shape=jax.ShapeDtypeStruct((NW * SENT, 2 * F), BF16),
        compiler_params=pltpu.CompilerParams(vmem_limit_bytes=58 << 20),
        name="whiten",
    )(order, slab, wid, raw, quality, dft_table())


def turn_block(wide, first, step, turned):
    for p in range(CB):
        t = wide[pl.ds(first + p, NW, stride=step), :].T
        turned[pl.ds(p, F, stride=2 * CB), :] = t[:F]
        turned[pl.ds(CB + p, F, stride=2 * CB), :] = t[F:]
    return turned[...].astype(BF16)


def turn_kernel(received, pair, own, wide, turned):
    wide[...] = received[...].astype(F32)
    for slot in range(2):
        block = turn_block(wide, slot * CB, SENT, turned)
        pair[pl.ds(slot * HALF_ROWS, HALF_ROWS), :] = block
        if slot == 0:
            own[...] = block


def turn(received):
    return pl.pallas_call(
        turn_kernel,
        in_specs=[pl.BlockSpec(memory_space=pltpu.VMEM)],
        out_specs=[pl.BlockSpec(memory_space=pltpu.VMEM)] * 2,
        out_shape=[
            jax.ShapeDtypeStruct((2 * HALF_ROWS, NW), BF16),
            jax.ShapeDtypeStruct((HALF_ROWS, NW), BF16),
        ],
        scratch_shapes=[pltpu.VMEM((NW * SENT, 2 * F), F32), pltpu.VMEM((HALF_ROWS, NW), F32)],
        compiler_params=pltpu.CompilerParams(vmem_limit_bytes=24 << 20),
        name="turn",
    )(received)


def shift(x, axis, amount):
    ids = np.arange(int(np.prod(GRID))).reshape(GRID)
    to = np.roll(ids, -amount, axis=axis)
    return lax.ppermute(x, AXES, [(int(a), int(b)) for a, b in zip(ids.ravel(), to.ravel())])


def gather_rings(pair, own):
    rows = [pair, shift(pair, Z, 1), shift(pair, Z, -1)]
    partner = shift(own, XL, 1)
    cols = []
    for block, far in ((own, 1), (partner, -1)):
        near = {way: shift(block, Y, way) for way in (1, -1)}
        cols += [block, near[1], near[-1], shift(near[far], Y, far)]
    rows.append(shift(rows[1][:HALF_ROWS], Z, 1))
    rows.append(shift(rows[2][HALF_ROWS:], Z, -1))
    others = [shift(pair, CORE, 1)]
    near = lax.optimization_barrier((*rows[1:3], *cols[1:3], *cols[5:7]))[:2]
    others += [shift(block, CORE, 1) for block in near]
    far = lax.optimization_barrier((*rows[3:], cols[3], cols[7]))[:2]
    others += [shift(block, CORE, 1) for block in far]
    return rows, others, cols


def block_offsets(wid):
    bits = lambda low, size: (wid >> low) & (size - 1)
    y, xl, z, xh, core = bits(5, 4), bits(4, 2), bits(2, 4), bits(1, 2), bits(0, 2)
    held = [(0, 0), (0, 1), (1, 0), (1, 1), (3, 0), (3, 1), (2, 0), (2, 1)]
    rows = [((z - ring) & 3) * 4 + (xh ^ flip) * 2 for ring, flip in held]
    cols = [((y - ring) & 3) * 2 + (xl ^ flip) for flip in (0, 1) for ring in (0, 1, 3, 2)]
    return [at * CB for at in [r + core for r in rows] + [r + 1 - core for r in rows] + cols]


def product_kernel(wid, *refs):
    rows, cols, (out, b, made, sent) = refs[:16], refs[16:24], refs[24:]
    step = pl.program_id(0)
    chunks = KC // OUT_BINS

    def send(slot, at):
        first = pl.multiple_of(at * KC + slot * OUT_BINS, OUT_BINS)
        return pltpu.make_async_copy(
            made.at[slot], out.at[:, pl.ds(first, OUT_BINS)], sent.at[slot]
        )

    offsets = [pl.multiple_of(at, CB) for at in block_offsets(wid[0])]
    for block, offset in zip(cols, offsets[16:]):
        re, im = block[:, 0:CB, :], block[:, CB : 2 * CB, :]
        b[:, pl.ds(offset, CB), 0:NW] = re
        b[:, pl.ds(offset, CB), NW : 2 * NW] = im
        b[:, pl.ds(128 + offset, CB), 0:NW] = -im
        b[:, pl.ds(128 + offset, CB), NW : 2 * NW] = re
    factor = 1.0 / math.sqrt(NW)
    for slot in range(chunks):
        pl.when(step > 0)(lambda slot=slot: send(slot, step - 1).wait())
        for bin_index in range(OUT_BINS):
            k = slot * OUT_BINS + bin_index
            parts = [
                jnp.concatenate([row[k, 0:CB, :], row[k, CB : 2 * CB, :]], axis=1) for row in rows
            ]
            o = lax.dot_general(
                jnp.concatenate(parts, axis=0),
                b[k],
                (((1,), (1,)), ((), ())),
                preferred_element_type=F32,
            )
            o = o * factor
            for index, offset in enumerate(offsets[:16]):
                part = o[index * CB : (index + 1) * CB]
                made[slot, 0, bin_index, pl.ds(offset, CB), :] = part[:, :128]
                made[slot, 1, bin_index, pl.ds(offset, CB), :] = part[:, 128:]
        send(slot, step).start()

    @pl.when(step == pl.num_programs(0) - 1)
    def _():
        for slot in range(chunks):
            send(slot, step).wait()


def product(wid, blocks):
    steps = F // KC
    arrays, specs = [], []
    for block in blocks:
        for half in range(block.shape[0] // HALF_ROWS):
            arrays.append(block.reshape(-1, 2 * CB, NW))
            index_map = lambda i, m, half=half: (i + half * steps, 0, 0)
            specs.append(pl.BlockSpec((KC, 2 * CB, NW), index_map))
    return pl.pallas_call(
        product_kernel,
        grid_spec=pltpu.PrefetchScalarGridSpec(
            num_scalar_prefetch=1,
            grid=(steps,),
            in_specs=specs,
            out_specs=pl.BlockSpec(memory_space=pl.ANY),
            scratch_shapes=[
                pltpu.VMEM((KC, 256, 256), BF16),
                pltpu.VMEM((KC // OUT_BINS, 2, OUT_BINS, 256, 128), F32),
                pltpu.SemaphoreType.DMA((KC // OUT_BINS,)),
            ],
        ),
        out_shape=jax.ShapeDtypeStruct((2, F, 256, 128), F32),
        compiler_params=pltpu.CompilerParams(vmem_limit_bytes=58 << 20),
        name="product",
    )(wid, *arrays)


def body(raw, quality, channel_order, slab_order):
    src, rcv = lax.axis_index("src"), lax.axis_index("rcv")
    wid = (src * 16 + rcv).astype(jnp.int32).reshape(1)
    spectra = whiten(raw, quality.reshape(16, 128), channel_order, slab_order, wid)
    received = lax.all_to_all(
        spectra.reshape(NW, SENT, 2 * F), AXES, split_axis=0, concat_axis=0, tiled=True
    )
    pair, own = turn(received.reshape(NW * SENT, 2 * F))
    rows, others, cols = gather_rings(pair, own)
    return product(wid, rows + others + cols)


def solution(mesh):
    in_specs = (P(("src", "rcv"), None, None), P(("src", "rcv"), None), P(), P())
    out_specs = P(None, None, "src", "rcv")
    return jax.shard_map(body, mesh=mesh, in_specs=in_specs, out_specs=out_specs, check_vma=False)
```

```python
import functools
import math

import jax
import jax.numpy as jnp
import ml_dtypes
import numpy as np
from jax import lax
from jax.experimental import pallas as pl
from jax.experimental.pallas import tpu as pltpu
from jax.sharding import PartitionSpec as P

C, WLEN, F, HALF, BAND, SLABS, WIN_SLAB, NW, CB = 2048, 512, 64, 12, 2, 4, 32, 128, 16
AXES = ("src", "rcv")
GRID = (4, 2, 4, 2, 2)
Y, XL, Z, XH, CORE = range(5)
BF16, F32 = jnp.bfloat16, jnp.float32
ROWS = 1024
GROUP = 16
KC = 32
OUT_BINS = 8
XH_BIT = 2
SENT = 2 * CB
HALF_ROWS = F * 2 * CB


def dft_table():
    n = np.arange(WLEN)[:, None]
    phase = 2.0 * math.pi / WLEN * (n * np.arange(1, F + 1)[None, :] % WLEN)
    table = np.concatenate([np.cos(phase), -np.sin(phase)], axis=1)
    return jnp.asarray(table.astype(ml_dtypes.bfloat16))


def iotas(shape):
    return lax.broadcasted_iota(jnp.int32, shape, 0), lax.broadcasted_iota(jnp.int32, shape, 1)


def make_tables(inside, sums):
    row, col = iotas((WLEN, WLEN))
    inside[...] = jnp.where(jnp.abs(row - col) <= HALF, 1.0, 0.0).astype(BF16)
    row, col = iotas((4 * F, 4 * F))
    same = ((row ^ col) & F) == 0
    near = (jnp.abs((row & (F - 1)) - (col & (F - 1))) <= BAND) | (col >= 2 * F)
    sums[...] = jnp.where(same & near, 1.0, 0.0).astype(BF16)


def inverse_count(length, half_width, period):
    place = iotas((1, length))[1] & (period - 1)
    upper = jnp.minimum(place + half_width + 1, period)
    return 1.0 / (upper - jnp.maximum(place - half_width, 0)).astype(F32)


def whiten_kernel(order, slab, wid, raw, quality, dft, out, white, placed, inside, sums):
    step = pl.program_id(0)
    pl.when(step == 0)(functools.partial(make_tables, inside, sums))
    x = raw[0].astype(F32)
    centred = x - jnp.sum(x, axis=1, keepdims=True) * (1.0 / WLEN)
    magnitude = jnp.abs(centred)
    level = jnp.sum(magnitude, axis=1, keepdims=True) * (1.0 / WLEN) + 1e-6
    window_sum = jnp.dot(magnitude.astype(BF16), inside[...], preferred_element_type=F32)
    normed = (centred / (window_sum * inverse_count(WLEN, HALF, WLEN) + 0.25 * level)).astype(BF16)
    spectrum = jnp.dot(normed, dft[...], preferred_element_type=F32)
    squares = spectrum * spectrum
    power = squares + pltpu.roll(squares, F, 1)
    high = power.astype(BF16)
    low = (power - high.astype(F32)).astype(BF16)
    both = jnp.dot(
        jnp.concatenate([high, low], axis=1), sums[...], preferred_element_type=F32
    )
    total = both[:, 2 * F :] * (1.0 / F) + 1e-6
    amplitude = jnp.float32(0.0)
    for age in range(SLABS):
        amplitude += jnp.where(
            slab[age] == wid[0] // WIN_SLAB, jnp.float32(0.5 ** (age / SLABS)), jnp.float32(0.0)
        )
    eye = (
        lax.broadcasted_iota(jnp.int32, (128, 128), 0)
        == lax.broadcasted_iota(jnp.int32, (128, 128), 1)
    )
    weights = []
    for part in range(ROWS // 128):
        row = quality[pl.ds(step * (ROWS // 128) + part, 1), :].astype(F32)
        weights.append(jnp.sum(jnp.where(eye, row, 0.0), axis=1, keepdims=True))
    weight = jnp.concatenate(weights, axis=0) * amplitude
    scale = weight * lax.rsqrt(both[:, : 2 * F] * inverse_count(2 * F, BAND, F) + 0.1 * total)
    white[pl.ds(pl.multiple_of(step * ROWS, ROWS), ROWS), :] = spectrum * scale

    @pl.when(step == pl.num_programs(0) - 1)
    def _():
        def place(group, carry):
            for u in range(GROUP):
                base = (group * GROUP + u) * CB
                for j in range(CB):
                    placed[pl.ds(u * CB + j, 1), :] = white[pl.ds(order[base + j], 1), :]
            for u in range(GROUP):
                owner = group * GROUP + u
                block = placed[pl.ds(u * CB, CB), :].astype(BF16)
                for slot, partner in enumerate((0, XH_BIT)):
                    at = (owner ^ partner) * SENT + slot * CB
                    out[pl.ds(pl.multiple_of(at, CB), CB), :] = block
            return carry

        lax.fori_loop(0, C // CB // GROUP, place, 0)


def whiten(raw, quality, order, slab, wid):
    whole = lambda shape: pl.BlockSpec(shape, lambda i, *_: (0, 0))
    return pl.pallas_call(
        whiten_kernel,
        grid_spec=pltpu.PrefetchScalarGridSpec(
            num_scalar_prefetch=3,
            grid=(C // ROWS,),
            in_specs=[
                pl.BlockSpec((1, ROWS, WLEN), lambda i, *_: (0, i, 0)),
                whole(quality.shape),
                whole((WLEN, 2 * F)),
            ],
            out_specs=whole((NW * SENT, 2 * F)),
            scratch_shapes=[
                pltpu.VMEM((C, 2 * F), F32),
                pltpu.VMEM((GROUP * CB, 2 * F), F32),
                pltpu.VMEM((WLEN, WLEN), BF16),
                pltpu.VMEM((4 * F, 4 * F), BF16),
            ],
        ),
        out_shape=jax.ShapeDtypeStruct((NW * SENT, 2 * F), BF16),
        compiler_params=pltpu.CompilerParams(vmem_limit_bytes=58 << 20),
        name="whiten",
    )(order, slab, wid, raw, quality, dft_table())


def turn_block(wide, first, step, turned):
    for p in range(CB):
        t = wide[pl.ds(first + p, NW, stride=step), :].T
        turned[pl.ds(p, F, stride=2 * CB), :] = t[:F]
        turned[pl.ds(CB + p, F, stride=2 * CB), :] = t[F:]
    return turned[...].astype(BF16)


def turn_kernel(received, pair, own, wide, turned):
    wide[...] = received[...].astype(F32)
    for slot in range(2):
        block = turn_block(wide, slot * CB, SENT, turned)
        pair[pl.ds(slot * HALF_ROWS, HALF_ROWS), :] = block
        if slot == 0:
            own[...] = block


def turn(received):
    return pl.pallas_call(
        turn_kernel,
        in_specs=[pl.BlockSpec(memory_space=pltpu.VMEM)],
        out_specs=[pl.BlockSpec(memory_space=pltpu.VMEM)] * 2,
        out_shape=[
            jax.ShapeDtypeStruct((2 * HALF_ROWS, NW), BF16),
            jax.ShapeDtypeStruct((HALF_ROWS, NW), BF16),
        ],
        scratch_shapes=[pltpu.VMEM((NW * SENT, 2 * F), F32), pltpu.VMEM((HALF_ROWS, NW), F32)],
        compiler_params=pltpu.CompilerParams(vmem_limit_bytes=24 << 20),
        name="turn",
    )(received)


def shift(x, axis, amount):
    ids = np.arange(int(np.prod(GRID))).reshape(GRID)
    to = np.roll(ids, -amount, axis=axis)
    return lax.ppermute(x, AXES, [(int(a), int(b)) for a, b in zip(ids.ravel(), to.ravel())])


def gather_rings(pair, own):
    rows = [pair, shift(pair, Z, 1), shift(pair, Z, -1)]
    partner = shift(own, XL, 1)
    cols = []
    for block, far in ((own, 1), (partner, -1)):
        near = {way: shift(block, Y, way) for way in (1, -1)}
        cols += [block, near[1], near[-1], shift(near[far], Y, far)]
    rows.append(shift(rows[1][:HALF_ROWS], Z, 1))
    rows.append(shift(rows[2][HALF_ROWS:], Z, -1))
    others = [shift(pair, CORE, 1)]
    near = lax.optimization_barrier((*rows[1:3], *cols[1:3], *cols[5:7]))[:2]
    others += [shift(block, CORE, 1) for block in near]
    far = lax.optimization_barrier((*rows[3:], cols[3], cols[7]))[:2]
    others += [shift(block, CORE, 1) for block in far]
    return rows, others, cols


def block_offsets(wid):
    bits = lambda low, size: (wid >> low) & (size - 1)
    y, xl, z, xh, core = bits(5, 4), bits(4, 2), bits(2, 4), bits(1, 2), bits(0, 2)
    held = [(0, 0), (0, 1), (1, 0), (1, 1), (3, 0), (3, 1), (2, 0), (2, 1)]
    rows = [((z - ring) & 3) * 4 + (xh ^ flip) * 2 for ring, flip in held]
    cols = [((y - ring) & 3) * 2 + (xl ^ flip) for flip in (0, 1) for ring in (0, 1, 3, 2)]
    return [at * CB for at in [r + core for r in rows] + [r + 1 - core for r in rows] + cols]


def product_kernel(wid, *refs):
    rows, cols, (out, b, made, sent) = refs[:16], refs[16:24], refs[24:]
    step = pl.program_id(0)
    chunks = KC // OUT_BINS

    def send(slot, at):
        first = pl.multiple_of(at * KC + slot * OUT_BINS, OUT_BINS)
        return pltpu.make_async_copy(
            made.at[slot], out.at[:, pl.ds(first, OUT_BINS)], sent.at[slot]
        )

    offsets = [pl.multiple_of(at, CB) for at in block_offsets(wid[0])]
    for block, offset in zip(cols, offsets[16:]):
        re, im = block[:, 0:CB, :], block[:, CB : 2 * CB, :]
        b[:, pl.ds(offset, CB), 0:NW] = re
        b[:, pl.ds(offset, CB), NW : 2 * NW] = im
        b[:, pl.ds(128 + offset, CB), 0:NW] = -im
        b[:, pl.ds(128 + offset, CB), NW : 2 * NW] = re
    factor = 1.0 / math.sqrt(NW)
    for slot in range(chunks):
        pl.when(step > 0)(lambda slot=slot: send(slot, step - 1).wait())
        for bin_index in range(OUT_BINS):
            k = slot * OUT_BINS + bin_index
            parts = [
                jnp.concatenate([row[k, 0:CB, :], row[k, CB : 2 * CB, :]], axis=1) for row in rows
            ]
            o = lax.dot_general(
                jnp.concatenate(parts, axis=0),
                b[k],
                (((1,), (1,)), ((), ())),
                preferred_element_type=F32,
            )
            o = o * factor
            for index, offset in enumerate(offsets[:16]):
                part = o[index * CB : (index + 1) * CB]
                made[slot, 0, bin_index, pl.ds(offset, CB), :] = part[:, :128]
                made[slot, 1, bin_index, pl.ds(offset, CB), :] = part[:, 128:]
        send(slot, step).start()

    @pl.when(step == pl.num_programs(0) - 1)
    def _():
        for slot in range(chunks):
            send(slot, step).wait()


def product(wid, blocks):
    steps = F // KC
    arrays, specs = [], []
    for block in blocks:
        for half in range(block.shape[0] // HALF_ROWS):
            arrays.append(block.reshape(-1, 2 * CB, NW))
            index_map = lambda i, m, half=half: (i + half * steps, 0, 0)
            specs.append(pl.BlockSpec((KC, 2 * CB, NW), index_map))
    return pl.pallas_call(
        product_kernel,
        grid_spec=pltpu.PrefetchScalarGridSpec(
            num_scalar_prefetch=1,
            grid=(steps,),
            in_specs=specs,
            out_specs=pl.BlockSpec(memory_space=pl.ANY),
            scratch_shapes=[
                pltpu.VMEM((KC, 256, 256), BF16),
                pltpu.VMEM((KC // OUT_BINS, 2, OUT_BINS, 256, 128), F32),
                pltpu.SemaphoreType.DMA((KC // OUT_BINS,)),
            ],
        ),
        out_shape=jax.ShapeDtypeStruct((2, F, 256, 128), F32),
        compiler_params=pltpu.CompilerParams(vmem_limit_bytes=36 << 20),
        name="product",
    )(wid, *arrays)


def body(raw, quality, channel_order, slab_order):
    src, rcv = lax.axis_index("src"), lax.axis_index("rcv")
    wid = (src * 16 + rcv).astype(jnp.int32).reshape(1)
    spectra = whiten(raw, quality.reshape(16, 128), channel_order, slab_order, wid)
    received = lax.all_to_all(
        spectra.reshape(NW, SENT, 2 * F), AXES, split_axis=0, concat_axis=0, tiled=True
    )
    pair, own = turn(received.reshape(NW * SENT, 2 * F))
    rows, others, cols = gather_rings(pair, own)
    return product(wid, rows + others + cols)


def solution(mesh):
    in_specs = (P(("src", "rcv"), None, None), P(("src", "rcv"), None), P(), P())
    out_specs = P(None, None, "src", "rcv")
    return jax.shard_map(body, mesh=mesh, in_specs=in_specs, out_specs=out_specs, check_vma=False)
```

```python
import functools
import math

import jax
import jax.numpy as jnp
import ml_dtypes
import numpy as np
from jax import lax
from jax.experimental import pallas as pl
from jax.experimental.pallas import tpu as pltpu
from jax.sharding import PartitionSpec as P

C, WLEN, F, HALF, BAND, SLABS, WIN_SLAB, NW, CB = 2048, 512, 64, 12, 2, 4, 32, 128, 16
AXES = ("src", "rcv")
GRID = (4, 2, 4, 2, 2)
Y, XL, Z, XH, CORE = range(5)
BF16, F32 = jnp.bfloat16, jnp.float32
ROWS = 1024
GROUP = 16
KC = 64
OUT_BINS = 8
XH_BIT = 2
SENT = 2 * CB
HALF_ROWS = F * 2 * CB


def dft_table():
    n = np.arange(WLEN)[:, None]
    phase = 2.0 * math.pi / WLEN * (n * np.arange(1, F + 1)[None, :] % WLEN)
    table = np.concatenate([np.cos(phase), -np.sin(phase)], axis=1)
    return jnp.asarray(table.astype(ml_dtypes.bfloat16))


def iotas(shape):
    return lax.broadcasted_iota(jnp.int32, shape, 0), lax.broadcasted_iota(jnp.int32, shape, 1)


def make_tables(inside, sums):
    row, col = iotas((WLEN, WLEN))
    inside[...] = jnp.where(jnp.abs(row - col) <= HALF, 1.0, 0.0).astype(BF16)
    row, col = iotas((4 * F, 4 * F))
    same = ((row ^ col) & F) == 0
    near = (jnp.abs((row & (F - 1)) - (col & (F - 1))) <= BAND) | (col >= 2 * F)
    sums[...] = jnp.where(same & near, 1.0, 0.0).astype(BF16)


def inverse_count(length, half_width, period):
    place = iotas((1, length))[1] & (period - 1)
    upper = jnp.minimum(place + half_width + 1, period)
    return 1.0 / (upper - jnp.maximum(place - half_width, 0)).astype(F32)


def whiten_kernel(order, slab, wid, raw, quality, dft, out, white, placed, inside, sums):
    step = pl.program_id(0)
    pl.when(step == 0)(functools.partial(make_tables, inside, sums))
    x = raw[0].astype(F32)
    centred = x - jnp.sum(x, axis=1, keepdims=True) * (1.0 / WLEN)
    magnitude = jnp.abs(centred)
    level = jnp.sum(magnitude, axis=1, keepdims=True) * (1.0 / WLEN) + 1e-6
    window_sum = jnp.dot(magnitude.astype(BF16), inside[...], preferred_element_type=F32)
    normed = (centred / (window_sum * inverse_count(WLEN, HALF, WLEN) + 0.25 * level)).astype(BF16)
    spectrum = jnp.dot(normed, dft[...], preferred_element_type=F32)
    squares = spectrum * spectrum
    power = squares + pltpu.roll(squares, F, 1)
    high = power.astype(BF16)
    low = (power - high.astype(F32)).astype(BF16)
    both = jnp.dot(
        jnp.concatenate([high, low], axis=1), sums[...], preferred_element_type=F32
    )
    total = both[:, 2 * F :] * (1.0 / F) + 1e-6
    amplitude = jnp.float32(0.0)
    for age in range(SLABS):
        amplitude += jnp.where(
            slab[age] == wid[0] // WIN_SLAB, jnp.float32(0.5 ** (age / SLABS)), jnp.float32(0.0)
        )
    eye = (
        lax.broadcasted_iota(jnp.int32, (128, 128), 0)
        == lax.broadcasted_iota(jnp.int32, (128, 128), 1)
    )
    weights = []
    for part in range(ROWS // 128):
        row = quality[pl.ds(step * (ROWS // 128) + part, 1), :].astype(F32)
        weights.append(jnp.sum(jnp.where(eye, row, 0.0), axis=1, keepdims=True))
    weight = jnp.concatenate(weights, axis=0) * amplitude
    scale = weight * lax.rsqrt(both[:, : 2 * F] * inverse_count(2 * F, BAND, F) + 0.1 * total)
    white[pl.ds(pl.multiple_of(step * ROWS, ROWS), ROWS), :] = spectrum * scale

    @pl.when(step == pl.num_programs(0) - 1)
    def _():
        def place(group, carry):
            for u in range(GROUP):
                base = (group * GROUP + u) * CB
                for j in range(CB):
                    placed[pl.ds(u * CB + j, 1), :] = white[pl.ds(order[base + j], 1), :]
            for u in range(GROUP):
                owner = group * GROUP + u
                block = placed[pl.ds(u * CB, CB), :].astype(BF16)
                for slot, partner in enumerate((0, XH_BIT)):
                    at = (owner ^ partner) * SENT + slot * CB
                    out[pl.ds(pl.multiple_of(at, CB), CB), :] = block
            return carry

        lax.fori_loop(0, C // CB // GROUP, place, 0)


def whiten(raw, quality, order, slab, wid):
    whole = lambda shape: pl.BlockSpec(shape, lambda i, *_: (0, 0))
    return pl.pallas_call(
        whiten_kernel,
        grid_spec=pltpu.PrefetchScalarGridSpec(
            num_scalar_prefetch=3,
            grid=(C // ROWS,),
            in_specs=[
                pl.BlockSpec((1, ROWS, WLEN), lambda i, *_: (0, i, 0)),
                whole(quality.shape),
                whole((WLEN, 2 * F)),
            ],
            out_specs=whole((NW * SENT, 2 * F)),
            scratch_shapes=[
                pltpu.VMEM((C, 2 * F), F32),
                pltpu.VMEM((GROUP * CB, 2 * F), F32),
                pltpu.VMEM((WLEN, WLEN), BF16),
                pltpu.VMEM((4 * F, 4 * F), BF16),
            ],
        ),
        out_shape=jax.ShapeDtypeStruct((NW * SENT, 2 * F), BF16),
        compiler_params=pltpu.CompilerParams(vmem_limit_bytes=58 << 20),
        name="whiten",
    )(order, slab, wid, raw, quality, dft_table())


def turn_block(wide, first, step, turned):
    for p in range(CB):
        t = wide[pl.ds(first + p, NW, stride=step), :].T
        turned[pl.ds(p, F, stride=2 * CB), :] = t[:F]
        turned[pl.ds(CB + p, F, stride=2 * CB), :] = t[F:]
    return turned[...].astype(BF16)


def turn_kernel(received, pair, own, wide, turned):
    wide[...] = received[...].astype(F32)
    for slot in range(2):
        block = turn_block(wide, slot * CB, SENT, turned)
        pair[pl.ds(slot * HALF_ROWS, HALF_ROWS), :] = block
        if slot == 0:
            own[...] = block


def turn(received):
    return pl.pallas_call(
        turn_kernel,
        in_specs=[pl.BlockSpec(memory_space=pltpu.VMEM)],
        out_specs=[pl.BlockSpec(memory_space=pltpu.VMEM)] * 2,
        out_shape=[
            jax.ShapeDtypeStruct((2 * HALF_ROWS, NW), BF16),
            jax.ShapeDtypeStruct((HALF_ROWS, NW), BF16),
        ],
        scratch_shapes=[pltpu.VMEM((NW * SENT, 2 * F), F32), pltpu.VMEM((HALF_ROWS, NW), F32)],
        compiler_params=pltpu.CompilerParams(vmem_limit_bytes=24 << 20),
        name="turn",
    )(received)


def shift(x, axis, amount):
    ids = np.arange(int(np.prod(GRID))).reshape(GRID)
    to = np.roll(ids, -amount, axis=axis)
    return lax.ppermute(x, AXES, [(int(a), int(b)) for a, b in zip(ids.ravel(), to.ravel())])


def gather_rings(pair, own):
    rows = [pair, shift(pair, Z, 1), shift(pair, Z, -1)]
    partner = shift(own, XL, 1)
    cols = []
    for block, far in ((own, 1), (partner, -1)):
        near = {way: shift(block, Y, way) for way in (1, -1)}
        cols += [block, near[1], near[-1], shift(near[far], Y, far)]
    rows.append(shift(rows[1][:HALF_ROWS], Z, 1))
    rows.append(shift(rows[2][HALF_ROWS:], Z, -1))
    others = [shift(pair, CORE, 1)]
    near = lax.optimization_barrier((*rows[1:3], *cols[1:3], *cols[5:7]))[:2]
    others += [shift(block, CORE, 1) for block in near]
    far = lax.optimization_barrier((*rows[3:], cols[3], cols[7]))[:2]
    others += [shift(block, CORE, 1) for block in far]
    return rows, others, cols


def block_offsets(wid):
    bits = lambda low, size: (wid >> low) & (size - 1)
    y, xl, z, xh, core = bits(5, 4), bits(4, 2), bits(2, 4), bits(1, 2), bits(0, 2)
    held = [(0, 0), (0, 1), (1, 0), (1, 1), (3, 0), (3, 1), (2, 0), (2, 1)]
    rows = [((z - ring) & 3) * 4 + (xh ^ flip) * 2 for ring, flip in held]
    cols = [((y - ring) & 3) * 2 + (xl ^ flip) for flip in (0, 1) for ring in (0, 1, 3, 2)]
    return [at * CB for at in [r + core for r in rows] + [r + 1 - core for r in rows] + cols]


def product_kernel(wid, *refs):
    blocks, (out, b, made, sent) = refs[:-4], refs[-4:]
    sides = [
        (block, half * F) for block in blocks for half in range(block.shape[0] // F)
    ]
    rows, cols = sides[:16], sides[16:]
    chunks = KC // OUT_BINS
    offsets = [pl.multiple_of(at, CB) for at in block_offsets(wid[0])]
    factor = 1.0 / math.sqrt(NW)

    def send(slot, at):
        first = pl.multiple_of(at * KC + slot * OUT_BINS, OUT_BINS)
        return pltpu.make_async_copy(
            made.at[slot], out.at[:, pl.ds(first, OUT_BINS)], sent.at[slot]
        )

    def some_bins(step, carry):
        first = step * KC
        for slot in range(chunks):
            for (block, base), offset in zip(cols, offsets[16:]):
                held = block[pl.ds(base + first + slot * OUT_BINS, OUT_BINS)]
                re, im = held[:, 0:CB, :], held[:, CB : 2 * CB, :]
                b[slot, :, pl.ds(offset, CB), 0:NW] = re
                b[slot, :, pl.ds(offset, CB), NW : 2 * NW] = im
                b[slot, :, pl.ds(128 + offset, CB), 0:NW] = -im
                b[slot, :, pl.ds(128 + offset, CB), NW : 2 * NW] = re
            for bin_index in range(OUT_BINS):
                k = slot * OUT_BINS + bin_index
                parts = []
                for block, base in rows:
                    held = block[base + first + k]
                    parts.append(jnp.concatenate([held[0:CB], held[CB : 2 * CB]], axis=1))
                o = lax.dot_general(
                    jnp.concatenate(parts, axis=0),
                    b[slot, bin_index],
                    (((1,), (1,)), ((), ())),
                    preferred_element_type=F32,
                )
                o = o * factor
                for index, offset in enumerate(offsets[:16]):
                    part = o[index * CB : (index + 1) * CB]
                    made[slot, 0, bin_index, pl.ds(offset, CB), :] = part[:, :128]
                    made[slot, 1, bin_index, pl.ds(offset, CB), :] = part[:, 128:]
            send(slot, step).start()
        return carry

    some_bins(0, 0)
    for slot in range(chunks):
        send(slot, F // KC - 1).wait()


def product(wid, blocks):
    arrays = [block.reshape(-1, 2 * CB, NW) for block in blocks]
    return pl.pallas_call(
        product_kernel,
        in_specs=[
            pl.BlockSpec(memory_space=pltpu.SMEM),
            *[pl.BlockSpec(memory_space=pltpu.VMEM) for _ in arrays],
        ],
        out_specs=pl.BlockSpec(memory_space=pl.ANY),
        scratch_shapes=[
            pltpu.VMEM((KC // OUT_BINS, OUT_BINS, 256, 256), BF16),
            pltpu.VMEM((KC // OUT_BINS, 2, OUT_BINS, 256, 128), F32),
            pltpu.SemaphoreType.DMA((KC // OUT_BINS,)),
        ],
        out_shape=jax.ShapeDtypeStruct((2, F, 256, 128), F32),
        compiler_params=pltpu.CompilerParams(vmem_limit_bytes=36 << 20),
        name="product",
    )(wid, *arrays)


def body(raw, quality, channel_order, slab_order):
    src, rcv = lax.axis_index("src"), lax.axis_index("rcv")
    wid = (src * 16 + rcv).astype(jnp.int32).reshape(1)
    spectra = whiten(raw, quality.reshape(16, 128), channel_order, slab_order, wid)
    received = lax.all_to_all(
        spectra.reshape(NW, SENT, 2 * F), AXES, split_axis=0, concat_axis=0, tiled=True
    )
    pair, own = turn(received.reshape(NW * SENT, 2 * F))
    rows, others, cols = gather_rings(pair, own)
    return product(wid, rows + others + cols)


def solution(mesh):
    in_specs = (P(("src", "rcv"), None, None), P(("src", "rcv"), None), P(), P())
    out_specs = P(None, None, "src", "rcv")
    return jax.shard_map(body, mesh=mesh, in_specs=in_specs, out_specs=out_specs, check_vma=False)
```

```python
import functools
import math

import jax
import jax.numpy as jnp
import ml_dtypes
import numpy as np
from jax import lax
from jax.experimental import pallas as pl
from jax.experimental.pallas import tpu as pltpu
from jax.sharding import PartitionSpec as P

C, WLEN, F, HALF, BAND, SLABS, WIN_SLAB, NW, CB = 2048, 512, 64, 12, 2, 4, 32, 128, 16
AXES = ("src", "rcv")
GRID = (4, 2, 4, 2, 2)
Y, XL, Z, XH, CORE = range(5)
BF16, F32 = jnp.bfloat16, jnp.float32
ROWS = 1024
GROUP = 16
KC = 64
OUT_BINS = 8
XH_BIT = 2
SENT = 2 * CB
HALF_ROWS = F * 2 * CB


def dft_table():
    n = np.arange(WLEN)[:, None]
    phase = 2.0 * math.pi / WLEN * (n * np.arange(1, F + 1)[None, :] % WLEN)
    table = np.concatenate([np.cos(phase), -np.sin(phase)], axis=1)
    return jnp.asarray(table.astype(ml_dtypes.bfloat16))


def iotas(shape):
    return lax.broadcasted_iota(jnp.int32, shape, 0), lax.broadcasted_iota(jnp.int32, shape, 1)


def make_tables(inside, sums):
    row, col = iotas((WLEN, WLEN))
    inside[...] = jnp.where(jnp.abs(row - col) <= HALF, 1.0, 0.0).astype(BF16)
    row, col = iotas((4 * F, 4 * F))
    same = ((row ^ col) & F) == 0
    near = (jnp.abs((row & (F - 1)) - (col & (F - 1))) <= BAND) | (col >= 2 * F)
    sums[...] = jnp.where(same & near, 1.0, 0.0).astype(BF16)


def inverse_count(length, half_width, period):
    place = iotas((1, length))[1] & (period - 1)
    upper = jnp.minimum(place + half_width + 1, period)
    return 1.0 / (upper - jnp.maximum(place - half_width, 0)).astype(F32)


def whiten_kernel(order, slab, wid, raw, quality, dft, out, white, placed, inside, sums):
    step = pl.program_id(0)
    pl.when(step == 0)(functools.partial(make_tables, inside, sums))
    x = raw[0].astype(F32)
    centred = x - jnp.sum(x, axis=1, keepdims=True) * (1.0 / WLEN)
    magnitude = jnp.abs(centred)
    level = jnp.sum(magnitude, axis=1, keepdims=True) * (1.0 / WLEN) + 1e-6
    window_sum = jnp.dot(magnitude.astype(BF16), inside[...], preferred_element_type=F32)
    normed = (centred / (window_sum * inverse_count(WLEN, HALF, WLEN) + 0.25 * level)).astype(BF16)
    spectrum = jnp.dot(normed, dft[...], preferred_element_type=F32)
    squares = spectrum * spectrum
    power = squares + pltpu.roll(squares, F, 1)
    high = power.astype(BF16)
    low = (power - high.astype(F32)).astype(BF16)
    both = jnp.dot(
        jnp.concatenate([high, low], axis=1), sums[...], preferred_element_type=F32
    )
    total = both[:, 2 * F :] * (1.0 / F) + 1e-6
    amplitude = jnp.float32(0.0)
    for age in range(SLABS):
        amplitude += jnp.where(
            slab[age] == wid[0] // WIN_SLAB, jnp.float32(0.5 ** (age / SLABS)), jnp.float32(0.0)
        )
    eye = (
        lax.broadcasted_iota(jnp.int32, (128, 128), 0)
        == lax.broadcasted_iota(jnp.int32, (128, 128), 1)
    )
    weights = []
    for part in range(ROWS // 128):
        row = quality[pl.ds(step * (ROWS // 128) + part, 1), :].astype(F32)
        weights.append(jnp.sum(jnp.where(eye, row, 0.0), axis=1, keepdims=True))
    weight = jnp.concatenate(weights, axis=0) * amplitude
    scale = weight * lax.rsqrt(both[:, : 2 * F] * inverse_count(2 * F, BAND, F) + 0.1 * total)
    white[pl.ds(pl.multiple_of(step * ROWS, ROWS), ROWS), :] = spectrum * scale

    @pl.when(step == pl.num_programs(0) - 1)
    def _():
        def place(group, carry):
            for u in range(GROUP):
                base = (group * GROUP + u) * CB
                for j in range(CB):
                    placed[pl.ds(u * CB + j, 1), :] = white[pl.ds(order[base + j], 1), :]
            for u in range(GROUP):
                owner = group * GROUP + u
                block = placed[pl.ds(u * CB, CB), :].astype(BF16)
                for slot, partner in enumerate((0, XH_BIT)):
                    at = (owner ^ partner) * SENT + slot * CB
                    out[pl.ds(pl.multiple_of(at, CB), CB), :] = block
            return carry

        lax.fori_loop(0, C // CB // GROUP, place, 0)


def whiten(raw, quality, order, slab, wid):
    whole = lambda shape: pl.BlockSpec(shape, lambda i, *_: (0, 0))
    return pl.pallas_call(
        whiten_kernel,
        grid_spec=pltpu.PrefetchScalarGridSpec(
            num_scalar_prefetch=3,
            grid=(C // ROWS,),
            in_specs=[
                pl.BlockSpec((1, ROWS, WLEN), lambda i, *_: (0, i, 0)),
                whole(quality.shape),
                whole((WLEN, 2 * F)),
            ],
            out_specs=whole((NW * SENT, 2 * F)),
            scratch_shapes=[
                pltpu.VMEM((C, 2 * F), F32),
                pltpu.VMEM((GROUP * CB, 2 * F), F32),
                pltpu.VMEM((WLEN, WLEN), BF16),
                pltpu.VMEM((4 * F, 4 * F), BF16),
            ],
        ),
        out_shape=jax.ShapeDtypeStruct((NW * SENT, 2 * F), BF16),
        compiler_params=pltpu.CompilerParams(vmem_limit_bytes=58 << 20),
        name="whiten",
    )(order, slab, wid, raw, quality, dft_table())


def turn_block(wide, first, step, turned):
    for p in range(CB):
        t = wide[pl.ds(first + p, NW, stride=step), :].T
        turned[pl.ds(p, F, stride=2 * CB), :] = t[:F]
        turned[pl.ds(CB + p, F, stride=2 * CB), :] = t[F:]
    return turned[...].astype(BF16)


def turn_own_kernel(received, own, wide, turned):
    wide[...] = received[:, 0:CB, :].astype(F32).reshape(wide.shape)
    own[...] = turn_block(wide, 0, CB, turned)


def turn_pair_kernel(received, own, pair, wide, turned):
    wide[...] = received[:, CB : 2 * CB, :].astype(F32).reshape(wide.shape)
    pair[0:HALF_ROWS, :] = own[...]
    pair[HALF_ROWS:, :] = turn_block(wide, 0, CB, turned)


def turn(kernel, rows, *operands):
    return pl.pallas_call(
        kernel,
        in_specs=[pl.BlockSpec(memory_space=pltpu.VMEM) for _ in operands],
        out_specs=pl.BlockSpec(memory_space=pltpu.VMEM),
        out_shape=jax.ShapeDtypeStruct((rows, NW), BF16),
        scratch_shapes=[pltpu.VMEM((NW * CB, 2 * F), F32), pltpu.VMEM((HALF_ROWS, NW), F32)],
        compiler_params=pltpu.CompilerParams(vmem_limit_bytes=24 << 20),
        name="turn",
    )(*operands)


def shift(x, axis, amount):
    ids = np.arange(int(np.prod(GRID))).reshape(GRID)
    to = np.roll(ids, -amount, axis=axis)
    return lax.ppermute(x, AXES, [(int(a), int(b)) for a, b in zip(ids.ravel(), to.ravel())])


def gather_rings(pair, own):
    rows = [pair, shift(pair, Z, 1), shift(pair, Z, -1)]
    partner = shift(own, XL, 1)
    cols = []
    for block, far in ((own, 1), (partner, -1)):
        near = {way: shift(block, Y, way) for way in (1, -1)}
        cols += [block, near[1], near[-1], shift(near[far], Y, far)]
    rows.append(shift(rows[1][:HALF_ROWS], Z, 1))
    rows.append(shift(rows[2][HALF_ROWS:], Z, -1))
    others = [shift(pair, CORE, 1)]
    near = lax.optimization_barrier((*rows[1:3], *cols[1:3], *cols[5:7]))[:2]
    others += [shift(block, CORE, 1) for block in near]
    far = lax.optimization_barrier((*rows[3:], cols[3], cols[7]))[:2]
    others += [shift(block, CORE, 1) for block in far]
    return rows, others, cols


def block_offsets(wid):
    bits = lambda low, size: (wid >> low) & (size - 1)
    y, xl, z, xh, core = bits(5, 4), bits(4, 2), bits(2, 4), bits(1, 2), bits(0, 2)
    held = [(0, 0), (0, 1), (1, 0), (1, 1), (3, 0), (3, 1), (2, 0), (2, 1)]
    rows = [((z - ring) & 3) * 4 + (xh ^ flip) * 2 for ring, flip in held]
    cols = [((y - ring) & 3) * 2 + (xl ^ flip) for flip in (0, 1) for ring in (0, 1, 3, 2)]
    return [at * CB for at in [r + core for r in rows] + [r + 1 - core for r in rows] + cols]


def product_kernel(wid, *refs):
    blocks, (out, b, made, sent) = refs[:-4], refs[-4:]
    sides = [
        (block, half * F) for block in blocks for half in range(block.shape[0] // F)
    ]
    rows, cols = sides[:16], sides[16:]
    chunks = KC // OUT_BINS
    offsets = [pl.multiple_of(at, CB) for at in block_offsets(wid[0])]
    factor = 1.0 / math.sqrt(NW)

    def send(slot, at):
        first = pl.multiple_of(at * KC + slot * OUT_BINS, OUT_BINS)
        return pltpu.make_async_copy(
            made.at[slot], out.at[:, pl.ds(first, OUT_BINS)], sent.at[slot]
        )

    def some_bins(step, carry):
        first = step * KC
        for slot in range(chunks):
            for (block, base), offset in zip(cols, offsets[16:]):
                held = block[pl.ds(base + first + slot * OUT_BINS, OUT_BINS)]
                re, im = held[:, 0:CB, :], held[:, CB : 2 * CB, :]
                b[slot, :, pl.ds(offset, CB), 0:NW] = re
                b[slot, :, pl.ds(offset, CB), NW : 2 * NW] = im
                b[slot, :, pl.ds(128 + offset, CB), 0:NW] = -im
                b[slot, :, pl.ds(128 + offset, CB), NW : 2 * NW] = re
            for bin_index in range(OUT_BINS):
                k = slot * OUT_BINS + bin_index
                parts = []
                for block, base in rows:
                    held = block[base + first + k]
                    parts.append(jnp.concatenate([held[0:CB], held[CB : 2 * CB]], axis=1))
                o = lax.dot_general(
                    jnp.concatenate(parts, axis=0),
                    b[slot, bin_index],
                    (((1,), (1,)), ((), ())),
                    preferred_element_type=F32,
                )
                o = o * factor
                for index, offset in enumerate(offsets[:16]):
                    part = o[index * CB : (index + 1) * CB]
                    made[slot, 0, bin_index, pl.ds(offset, CB), :] = part[:, :128]
                    made[slot, 1, bin_index, pl.ds(offset, CB), :] = part[:, 128:]
            send(slot, step).start()
        return carry

    some_bins(0, 0)
    for slot in range(chunks):
        send(slot, F // KC - 1).wait()


def product(wid, blocks):
    arrays = [block.reshape(-1, 2 * CB, NW) for block in blocks]
    return pl.pallas_call(
        product_kernel,
        in_specs=[
            pl.BlockSpec(memory_space=pltpu.SMEM),
            *[pl.BlockSpec(memory_space=pltpu.VMEM) for _ in arrays],
        ],
        out_specs=pl.BlockSpec(memory_space=pl.ANY),
        scratch_shapes=[
            pltpu.VMEM((KC // OUT_BINS, OUT_BINS, 256, 256), BF16),
            pltpu.VMEM((KC // OUT_BINS, 2, OUT_BINS, 256, 128), F32),
            pltpu.SemaphoreType.DMA((KC // OUT_BINS,)),
        ],
        out_shape=jax.ShapeDtypeStruct((2, F, 256, 128), F32),
        compiler_params=pltpu.CompilerParams(vmem_limit_bytes=36 << 20),
        name="product",
    )(wid, *arrays)


def body(raw, quality, channel_order, slab_order):
    src, rcv = lax.axis_index("src"), lax.axis_index("rcv")
    wid = (src * 16 + rcv).astype(jnp.int32).reshape(1)
    spectra = whiten(raw, quality.reshape(16, 128), channel_order, slab_order, wid)
    received = lax.all_to_all(
        spectra.reshape(NW, SENT, 2 * F), AXES, split_axis=0, concat_axis=0, tiled=True
    )
    own = turn(turn_own_kernel, HALF_ROWS, received)
    pair = turn(turn_pair_kernel, 2 * HALF_ROWS, received, own)
    rows, others, cols = gather_rings(pair, own)
    return product(wid, rows + others + cols)


def solution(mesh):
    in_specs = (P(("src", "rcv"), None, None), P(("src", "rcv"), None), P(), P())
    out_specs = P(None, None, "src", "rcv")
    return jax.shard_map(body, mesh=mesh, in_specs=in_specs, out_specs=out_specs, check_vma=False)
```
